128 devices in a mesh: space: 32 (over y, z, core), param: 4 (over x).
Axes of the slice: x: 4, y: 4, z: 4, core: 2. Of those that a mesh axis runs over, the one named last changes fastest.
Arguments:
- snapshots: float32 [196608, 4096], P('space', 'param'), may hold values from -1800 to 1800
- sketch: float32 [4096, 32], P('param'), may hold values from -0.09375 to 0.09375
- sketch_next: float32 [256, 32], replicated, may hold values from -0.375 to 0.375
Outputs:
- first_core: float32 [32, 196608], P(None, 'space')
- second_core: float32 [32, 512], P(None, 'param')
- remainder: float32 [32, 256], replicated
The draws below stay inside these ranges and needn't reach their ends.
All inputs are finite; a program needn't handle non-finite values.
Results may differ from the reference program's by a relative error of at most 0.00016.
Values sent between devices are 32-bit elements; how exact they have to be, the bound alone decides.
A program may use at most 128 MiB of HBM per device.

```python
import math
import jax
import jax.numpy as jnp
from jax import lax

R = 32
N1 = 16
N2 = 16
N3 = 16
ITERS = 3
C = 4096
ROWS = 196608


def draw_snapshots(key, part):
    key_values = jax.random.fold_in(key, 11)
    key_rows = jax.random.fold_in(key, 12)
    key_cols = jax.random.fold_in(key, 13)
    row_scale = jnp.exp(jax.random.uniform(key_rows, (ROWS, 1), jnp.float32) * math.log(10.0))
    ramp = 1.0 + 2.0 * jnp.arange(ROWS, dtype=jnp.float32)[:, None] / ROWS
    col_scale = jnp.exp(jax.random.uniform(key_cols, (1, C), jnp.float32) * math.log(10.0))
    values = jax.random.truncated_normal(key_values, -6.0, 6.0, (ROWS, C), jnp.float32)
    return (values * row_scale * ramp * col_scale).astype(jnp.float32)


def shard_levels(stream_key, extent, cuts, least, high):
    def one(position, blocks):
        steps = jax.random.uniform(jax.random.fold_in(jax.random.fold_in(stream_key, 6), position), (blocks,), jnp.float32, least / len(cuts), high / len(cuts))
        return jnp.repeat(jnp.exp(steps), extent[position] // blocks).reshape((-1,) + (1,) * (len(extent) - position - 1))

    loudness = one(*cuts[0])
    for cut in cuts[1:]:
        loudness = loudness * one(*cut)
    return loudness


def noise(rng, dims, spread, reach, pieces=(), kind=jnp.bfloat16):
    array = jax.random.normal(rng, dims, jnp.float32) * spread
    if len(pieces) > 0:
        array = shard_levels(rng, dims, pieces, -0.22, 0.18) * array
    return jnp.clip(array, min=-reach, max=reach).astype(kind)


def setup_inputs(seed: int = 0) -> dict:
    streams_of = jax.random.split(jax.random.key(seed), 4)
    return {
        "snapshots": draw_snapshots(jax.random.fold_in(streams_of[3], 71), 0),
        "sketch": noise(streams_of[1], (C, R), C ** -0.5, 0.09375, ((0, 4),), jnp.float32),
        "sketch_next": noise(streams_of[2], (N2 * N3, R), (N2 * N3) ** -0.5, 0.375, (), jnp.float32),
    }


def frame(block):
    highest = lax.Precision.HIGHEST
    gram_matrix = jnp.dot(block, block.T, precision=highest)
    lower = jnp.linalg.cholesky(gram_matrix)
    return jax.scipy.linalg.solve_triangular(lower, block, lower=True)

def reference(snapshots, sketch, sketch_next):
    highest = lax.Precision.HIGHEST
    sketched = lax.dot_general(sketch, snapshots, (((0,), (1,)), ((), ())), precision=highest)
    basis = frame(sketched)
    for step in range(ITERS):
        across = jnp.dot(basis, snapshots, precision=highest)
        column_frame = frame(across)
        sketched = lax.dot_general(column_frame, snapshots, (((1,), (1,)), ((), ())), precision=highest)
        basis = frame(sketched)
    coefficients = jnp.dot(basis, snapshots, precision=highest) / math.sqrt(ROWS)
    unfold = coefficients.reshape(R, N1, N2 * N3).transpose(1, 0, 2).reshape(N1 * R, N2 * N3)
    second_sketch = lax.dot_general(sketch_next, unfold, (((0,), (1,)), ((), ())), precision=highest)
    second_frame = frame(second_sketch)
    remainder = jnp.dot(second_frame, unfold, precision=highest) / math.sqrt(R * N1)
    return (basis * math.sqrt(ROWS), second_frame * math.sqrt(R * N1), remainder)
```

```python
import functools
import math

import jax
import jax.numpy as jnp
from jax import lax
from jax.experimental import pallas as pl
from jax.experimental.pallas import tpu as pltpu
from jax.sharding import PartitionSpec as P

MESH = pl.DeviceIdType.MESH
R = 32
MODES = 256
ITERS = 3
F32, BF16 = jnp.float32, jnp.bfloat16
NN = (((1,), (0,)), ((), ()))
NT = (((1,), (1,)), ((), ()))


def exact(a, b, dims=NN):
    return lax.dot_general(a, b, dims, precision=lax.Precision.HIGHEST, preferred_element_type=F32)


def split(value):
    high = value.astype(BF16)
    low = (value - high.astype(F32)).astype(BF16)
    return jnp.concatenate([high, low], axis=0)


def fold(pair):
    return pair[:R] + pair[R:]


def gram_of(stacked):
    both = lax.dot_general(stacked, stacked, NT, preferred_element_type=F32)
    half = fold(both)
    return half[:, :R] + half[:, R:]


def inverse_factor(gram):
    rows = lax.broadcasted_iota(jnp.int32, (R, R), 0)
    columns = lax.broadcasted_iota(jnp.int32, (R, R), 1)
    eye = jnp.where(rows == columns, 1.0, 0.0).astype(F32)
    work = jnp.concatenate([gram, eye], axis=1)
    below = lax.broadcasted_iota(jnp.int32, (R, 2 * R), 0)
    for j in range(R - 1):
        row = work[j : j + 1, :]
        scaled = row / row[:, j : j + 1]
        work = work - jnp.where(below > j, work[:, j : j + 1], 0.0) * scaled
    diagonal = jnp.sum(jnp.where(rows == columns, work[:, :R], 0.0), axis=1, keepdims=True)
    return work[:, R:] / jnp.sqrt(diagonal)


def pack(square):
    return jnp.concatenate([square[8 * i : 8 * i + 8] for i in range(4)], axis=1)


def unpack(tile):
    return jnp.concatenate([tile[:, R * i : R * i + R] for i in range(4)], axis=0)


def kernel(
    ns, nx, total_rows, unfold_rows,
    snap, sketch, following, basis_out, second_out, rest_out,
    high, low, stage, zst, ypart, first_in, second_in, yfull, zacc, zfull,
    tiles_out, tiles_in, sums, gram_out, gram_in, last_out, last_in,
    factor_z, factor_y,
    load_sem, send_sem, recv_sem, tile_send, tile_recv, sum_send, sum_recv,
    gram_send, gram_recv, last_send, last_recv, out_sem,
):
    me, mx = lax.axis_index("space"), lax.axis_index("param")
    right, left, across = lax.rem(mx + 1, nx), lax.rem(mx + nx - 1, nx), lax.rem(mx + 2, nx)
    halves, hrows, columns = high.shape
    per = tiles_out.shape[1] - 1

    def part(quarter, half):
        return quarter * 2 + half

    order = [
        part(across, 0), part(across, 1), part(right, 1), part(left, 0),
        part(right, 0), part(left, 1), part(mx, 0), part(mx, 1),
    ]

    def load(n):
        return pltpu.make_async_copy(
            snap.at[pl.ds(pl.multiple_of(order[n] * hrows, 256), hrows), :],
            stage.at[n % 2], load_sem.at[n % 2],
        )

    load(0).start()
    load(1).start()

    barrier = pltpu.get_barrier_semaphore()

    def greet(d, carry):
        pl.semaphore_signal(barrier, inc=1, device_id=(lax.rem(me + d, ns), mx), device_id_type=MESH)
        return carry

    lax.fori_loop(1, ns, greet, 0)
    for d in range(1, nx):
        pl.semaphore_signal(barrier, inc=1, device_id=(me, lax.rem(mx + d, nx)), device_id_type=MESH)

    zst[...] = split(sketch[...].T)
    factor_z[...] = jnp.where(
        lax.broadcasted_iota(jnp.int32, (R, R), 0) == lax.broadcasted_iota(jnp.int32, (R, R), 1), 1.0, 0.0
    ).astype(F32)
    pl.semaphore_wait(barrier, ns - 1 + nx - 1)

    def compute(it, n):
        h = order[n]

        @pl.when(it == 0)
        def _():
            load(n).wait()

            def cut(i, carry):
                at = pl.ds(pl.multiple_of(i * 16, 16), 16)
                value = stage[n % 2, at, :]
                top = value.astype(BF16)
                high[h, at, :] = top
                low[h, at, :] = (value - top.astype(F32)).astype(BF16)
                return carry

            lax.fori_loop(0, hrows // 16, cut, 0)
            if n + 2 < halves:
                load(n + 2).start()

        for b in range(hrows // 256):
            at = pl.ds(b * 256, 256)
            pair = lax.dot_general(zst[...], high[h, at, :], NT, preferred_element_type=F32)
            pair += lax.dot_general(zst[...], low[h, at, :], NT, preferred_element_type=F32)
            ypart[h, :, at] = fold(pair)

    def along_x(source, target, n, it, x):
        return pltpu.make_async_remote_copy(
            src_ref=source, dst_ref=target, send_sem=send_sem.at[n], recv_sem=recv_sem.at[it, n],
            device_id=(me, x), device_id_type=MESH,
        )

    def accumulate(it, h):
        stacked = split(yfull[it, h])
        for b in range(columns // 256):
            at = pl.ds(b * 256, 256)
            pair = lax.dot_general(stacked, high[h, :, at], NN, preferred_element_type=F32)
            pair += lax.dot_general(stacked, low[h, :, at], NN, preferred_element_type=F32)
            zacc[:, at] += fold(pair)
        return gram_of(stacked)

    def gram_copy(it, d):
        return pltpu.make_async_remote_copy(
            src_ref=gram_out, dst_ref=gram_in.at[it, mx], send_sem=gram_send.at[d - 1], recv_sem=gram_recv.at[it, d - 1],
            device_id=(me, lax.rem(mx + d, nx)), device_id_type=MESH,
        )

    def iteration(it, carry):
        compute(it, 0)
        a_right = along_x(ypart.at[order[0]], first_in.at[it, 0], 0, it, right)
        a_right.start()
        compute(it, 1)
        a_left = along_x(ypart.at[order[1]], first_in.at[it, 1], 1, it, left)
        a_left.start()
        compute(it, 2)
        b_right = along_x(ypart.at[order[2]], second_in.at[it, 0, 1], 2, it, right)
        b_right.start()
        compute(it, 3)
        b_left = along_x(ypart.at[order[3]], second_in.at[it, 1, 0], 3, it, left)
        b_left.start()
        compute(it, 4)
        a_right.wait_recv()
        ypart[order[4]] += first_in[it, 0]
        c_right = along_x(ypart.at[order[4]], second_in.at[it, 0, 0], 4, it, right)
        c_right.start()
        compute(it, 5)
        a_left.wait_recv()
        ypart[order[5]] += first_in[it, 1]
        c_left = along_x(ypart.at[order[5]], second_in.at[it, 1, 1], 5, it, left)
        c_left.start()
        compute(it, 6)
        compute(it, 7)

        @pl.when(it > 0)
        def _():
            for d in range(1, nx):
                gram_copy(it - 1, d).wait()
            total = gram_in[it - 1, 0]
            for x in range(1, nx):
                total = total + gram_in[it - 1, x]
            factor_z[...] = inverse_factor(unpack(total))

        def finish(half):
            h = part(mx, half)
            value = ypart[h] + second_in[it, 0, half] + second_in[it, 1, half]
            yfull[it, h] = exact(factor_z[...], value)

        def to_right(h, n):
            return along_x(yfull.at[it, h], yfull.at[it, h], n, it, right)

        def to_left(h, n):
            return along_x(yfull.at[it, h], yfull.at[it, h], n, it, left)

        c_right.wait_recv()
        b_left.wait_recv()
        finish(0)
        own0_right = to_right(part(mx, 0), 6)
        own0_right.start()
        own0_left = to_left(part(mx, 0), 7)
        own0_left.start()
        b_right.wait_recv()
        c_left.wait_recv()
        finish(1)
        own1_left = to_left(part(mx, 1), 8)
        own1_left.start()
        own1_right = to_right(part(mx, 1), 9)
        own1_right.start()

        zacc[...] = jnp.zeros_like(zacc)
        gram = accumulate(it, part(mx, 0))
        gram = gram + accumulate(it, part(mx, 1))
        own0_right.wait_recv()
        on_right = to_right(part(left, 0), 10)
        on_right.start()
        own1_left.wait_recv()
        on_left = to_left(part(right, 1), 11)
        on_left.start()
        gram = gram + accumulate(it, part(left, 0))
        gram = gram + accumulate(it, part(right, 1))
        own0_left.wait_recv()
        gram = gram + accumulate(it, part(right, 0))
        own1_right.wait_recv()
        gram = gram + accumulate(it, part(left, 1))
        on_right.wait_recv()
        gram = gram + accumulate(it, part(across, 0))
        on_left.wait_recv()
        gram = gram + accumulate(it, part(across, 1))

        packed = pack(gram)
        for g in range(columns // 128):
            block = zacc[:, pl.ds(g * 128, 128)].reshape(4, 8, 128)
            for t in range(4):
                tiles_out[(g * 4 + t) // per, (g * 4 + t) % per] = block[t]

        def place(s, carry):
            tiles_out[s, per] = packed
            return carry

        lax.fori_loop(0, ns, place, 0)
        tiles_in[it, me] = tiles_out[me]

        def tile_copy(d):
            s = lax.rem(me + d, ns)
            return pltpu.make_async_remote_copy(
                src_ref=tiles_out.at[s], dst_ref=tiles_in.at[it, me], send_sem=tile_send, recv_sem=tile_recv.at[it],
                device_id=(s, mx), device_id_type=MESH,
            )

        def sum_copy(d):
            s = lax.rem(me + d, ns)
            return pltpu.make_async_remote_copy(
                src_ref=sums.at[it, me], dst_ref=sums.at[it, me], send_sem=sum_send, recv_sem=sum_recv.at[it],
                device_id=(s, mx), device_id_type=MESH,
            )

        def start(copy):
            def go(d, carry):
                copy(d).start()
                return carry

            lax.fori_loop(1, ns, go, 0)

        def all_but_one(ref, sem):
            some = ref.at[it, pl.ds(0, ns - 1)]
            pltpu.make_async_copy(some, some, sem).wait()

        start(tile_copy)
        for copy in (a_right, a_left, b_right, b_left, c_right, c_left):
            copy.wait_send()
        for copy in (own0_right, own0_left, own1_left, own1_right, on_right, on_left):
            copy.wait_send()
        all_but_one(tiles_in, tile_recv.at[it])

        def add(s, carry):
            return carry + tiles_in[it, s]

        total = lax.fori_loop(1, ns, add, tiles_in[it, 0])
        sums[it, me] = total[:per]
        start(sum_copy)
        factor_y[...] = inverse_factor(unpack(total[per]))
        all_but_one(tiles_in, tile_send)
        all_but_one(sums, sum_recv.at[it])
        all_but_one(sums, sum_send)
        gathered = sums[it].reshape(R, 8, 128)
        for g in range(columns // 128):
            block = gathered[g * 4 : g * 4 + 4].reshape(R, 128)
            zfull[:, g * 128 : g * 128 + 128] = exact(factor_y[...], block)

        @pl.when(it < ITERS)
        def _():
            stacked = split(zfull[...])
            zst[...] = stacked
            mine = pack(gram_of(stacked))
            gram_out[...] = mine
            gram_in[it, mx] = mine
            for d in range(1, nx):
                gram_copy(it, d).start()

        return carry

    lax.fori_loop(0, ITERS + 1, iteration, 0)

    turned = following[...].T
    slices = columns // MODES
    zfull[...] = zfull[...] * (1.0 / math.sqrt(total_rows))
    sketched, rest = [], jnp.zeros((R, MODES), F32)
    for i in range(slices):
        block = zfull[:, pl.ds(i * MODES, MODES)]
        one = exact(turned, block, NT)
        rest = rest + exact(one, block)
        sketched.append(one)
    sketched = jnp.concatenate(sketched, axis=1)
    last_out[:, pl.ds(0, MODES)] = rest
    last_out[:, pl.ds(MODES, 128)] = jnp.concatenate(
        [exact(sketched, sketched, NT), jnp.zeros((R, 128 - R), F32)], axis=1
    )
    last_in[mx] = last_out[...]

    def last_copy(d):
        return pltpu.make_async_remote_copy(
            src_ref=last_out, dst_ref=last_in.at[mx], send_sem=last_send.at[d - 1], recv_sem=last_recv.at[d - 1],
            device_id=(me, lax.rem(mx + d, nx)), device_id_type=MESH,
        )

    for d in range(1, nx):
        last_copy(d).start()

    def write(h):
        return pltpu.make_async_copy(
            ypart.at[h], basis_out.at[:, pl.ds(h * hrows, hrows)], out_sem.at[h]
        )

    for h in range(halves):
        ypart[h] = exact(factor_y[...], yfull[ITERS, h]) * math.sqrt(total_rows)
        write(h).start()

    for d in range(1, nx):
        last_copy(d).wait()
    total = last_in[0]
    for x in range(1, nx):
        total = total + last_in[x]
    factor = inverse_factor(total[:, MODES : MODES + R])
    second_out[...] = exact(factor, sketched) * math.sqrt(unfold_rows)
    rest_out[...] = exact(factor, total[:, :MODES]) / math.sqrt(unfold_rows)
    for h in range(halves):
        write(h).wait()


def solution(mesh):
    ns, nx = mesh.shape["space"], mesh.shape["param"]

    def shards(snapshots, sketch, following):
        rows, columns = snapshots.shape
        hrows = rows // (2 * nx)
        per = R // ns
        slices = columns // MODES
        steps = ITERS + 1
        dma = pltpu.SemaphoreType.DMA
        return pl.pallas_call(
            functools.partial(kernel, ns, nx, rows * ns, slices * R * nx),
            out_shape=(
                jax.ShapeDtypeStruct((R, rows), F32),
                jax.ShapeDtypeStruct((R, slices * R), F32),
                jax.ShapeDtypeStruct((R, MODES), F32),
            ),
            in_specs=[
                pl.BlockSpec(memory_space=pl.ANY),
                pl.BlockSpec(memory_space=pltpu.VMEM),
                pl.BlockSpec(memory_space=pltpu.VMEM),
            ],
            out_specs=(
                pl.BlockSpec(memory_space=pl.ANY),
                pl.BlockSpec(memory_space=pltpu.VMEM),
                pl.BlockSpec(memory_space=pltpu.VMEM),
            ),
            scratch_shapes=[
                pltpu.VMEM((2 * nx, hrows, columns), BF16),
                pltpu.VMEM((2 * nx, hrows, columns), BF16),
                pltpu.VMEM((2, hrows, columns), F32),
                pltpu.VMEM((2 * R, columns), BF16),
                pltpu.VMEM((2 * nx, R, hrows), F32),
                pltpu.VMEM((steps, 2, R, hrows), F32),
                pltpu.VMEM((steps, 2, 2, R, hrows), F32),
                pltpu.VMEM((steps, 2 * nx, R, hrows), F32),
                pltpu.VMEM((R, columns), F32),
                pltpu.VMEM((R, columns), F32),
                pltpu.VMEM((ns, per + 1, 8, 128), F32),
                pltpu.VMEM((steps, ns, per + 1, 8, 128), F32),
                pltpu.VMEM((steps, ns, per, 8, 128), F32),
                pltpu.VMEM((8, 128), F32),
                pltpu.VMEM((steps, nx, 8, 128), F32),
                pltpu.VMEM((R, MODES + 128), F32),
                pltpu.VMEM((nx, R, MODES + 128), F32),
                pltpu.VMEM((R, R), F32),
                pltpu.VMEM((R, R), F32),
                dma((2,)),
                dma((12,)),
                dma((steps, 12)),
                dma,
                dma((steps,)),
                dma,
                dma((steps,)),
                dma((nx - 1,)),
                dma((steps, nx - 1)),
                dma((nx - 1,)),
                dma((nx - 1,)),
                dma((2 * nx,)),
            ],
            compiler_params=pltpu.CompilerParams(
                collective_id=0, has_side_effects=True, vmem_limit_bytes=60 * 1024 * 1024
            ),
        )(snapshots, sketch, following)

    return jax.shard_map(
        shards,
        mesh=mesh,
        in_specs=(P("space", "param"), P("param", None), P()),
        out_specs=(P(None, "space"), P(None, "param"), P()),
        check_vma=False,
    )
```

```python
import functools
import math

import jax
import jax.numpy as jnp
from jax import lax
from jax.experimental import pallas as pl
from jax.experimental.pallas import tpu as pltpu
from jax.sharding import PartitionSpec as P

MESH = pl.DeviceIdType.MESH
R = 32
MODES = 256
ITERS = 3
PIECES = 6
F32, BF16 = jnp.float32, jnp.bfloat16
NN = (((1,), (0,)), ((), ()))
NT = (((1,), (1,)), ((), ()))


def exact(a, b, dims=NN):
    return lax.dot_general(a, b, dims, precision=lax.Precision.HIGHEST, preferred_element_type=F32)


def split(value):
    high = value.astype(BF16)
    low = (value - high.astype(F32)).astype(BF16)
    return jnp.concatenate([high, low], axis=0)


def fold(pair):
    return pair[:R] + pair[R:]


def gram_of(stacked):
    both = lax.dot_general(stacked, stacked, NT, preferred_element_type=F32)
    half = fold(both)
    return half[:, :R] + half[:, R:]


def inverse_factor(gram):
    rows = lax.broadcasted_iota(jnp.int32, (R, R), 0)
    columns = lax.broadcasted_iota(jnp.int32, (R, R), 1)
    eye = jnp.where(rows == columns, 1.0, 0.0).astype(F32)
    work = jnp.concatenate([gram, eye], axis=1)
    below = lax.broadcasted_iota(jnp.int32, (R, 2 * R), 0)
    for j in range(R - 1):
        row = work[j : j + 1, :]
        scaled = row / row[:, j : j + 1]
        work = work - jnp.where(below > j, work[:, j : j + 1], 0.0) * scaled
    diagonal = jnp.sum(jnp.where(rows == columns, work[:, :R], 0.0), axis=1, keepdims=True)
    return work[:, R:] / jnp.sqrt(diagonal)


def pack(square):
    return jnp.concatenate([square[8 * i : 8 * i + 8] for i in range(4)], axis=1)


def unpack(tile):
    return jnp.concatenate([tile[:, R * i : R * i + R] for i in range(4)], axis=0)


def kernel(
    ns, nx, total_rows, unfold_rows,
    snap, sketch, following, basis_out, second_out, rest_out,
    high, low, stage, zst, ypart, first_in, second_in, yfull, zacc, zfull,
    tiles_out, tiles_in, sums, gram_in, own_in, space_in, last_out, last_in,
    factor_z, factor_y,
    load_sem, send_sem, recv_sem, tile_send, tile_recv, sum_send, sum_recv,
    gram_send, gram_recv, own_send, own_recv, space_send, space_recv, last_send, last_recv, out_sem,
):
    me, mx = lax.axis_index("space"), lax.axis_index("param")
    right, left, across = lax.rem(mx + 1, nx), lax.rem(mx + nx - 1, nx), lax.rem(mx + 2, nx)
    pieces, prows, columns = high.shape
    per = tiles_out.shape[1]
    third = PIECES // 2
    loads = stage.shape[0]

    def part(quarter, piece):
        return quarter * PIECES + piece

    steps = range(third)
    far = [part(across, k + side * third) for k in steps for side in (0, 1)]
    plain = [h for k in steps for h in (part(right, k + third), part(left, k))]
    merged = [h for k in steps for h in (part(right, k), part(left, k + third))]
    own = [part(mx, k + side * third) for k in steps for side in (0, 1)]
    order = far + plain + merged + own

    def load(n):
        return pltpu.make_async_copy(
            snap.at[pl.ds(pl.multiple_of(order[n] * prows, prows), prows), :],
            stage.at[n % loads], load_sem.at[n % loads],
        )

    for n in range(loads):
        load(n).start()

    barrier = pltpu.get_barrier_semaphore()

    def greet(d, carry):
        pl.semaphore_signal(barrier, inc=1, device_id=(lax.rem(me + d, ns), mx), device_id_type=MESH)
        return carry

    lax.fori_loop(1, ns, greet, 0)
    for d in range(1, nx):
        pl.semaphore_signal(barrier, inc=1, device_id=(me, lax.rem(mx + d, nx)), device_id_type=MESH)

    zst[...] = split(sketch[...])
    eye = jnp.where(
        lax.broadcasted_iota(jnp.int32, (R, R), 0) == lax.broadcasted_iota(jnp.int32, (R, R), 1), 1.0, 0.0
    ).astype(F32)
    for x in range(nx):
        gram_in[0, x] = pack(eye * (1.0 / nx))
    pl.semaphore_wait(barrier, ns - 1 + nx - 1)

    def fetch(n):
        load(n).wait()

        def cut(i, carry):
            at = pl.ds(pl.multiple_of(i * 16, 16), 16)
            value = stage[n % loads, at, :]
            top = value.astype(BF16)
            high[order[n], at, :] = top
            low[order[n], at, :] = (value - top.astype(F32)).astype(BF16)
            return carry

        lax.fori_loop(0, prows // 16, cut, 0)
        if n + loads < pieces:
            load(n + loads).start()

    def product(n):
        h = order[n]
        pair = lax.dot_general(zst[...], high[h], NT, preferred_element_type=F32)
        pair += lax.dot_general(zst[...], low[h], NT, preferred_element_type=F32)
        return fold(pair)

    def compute(it, n):
        pl.when(it == 0)(lambda: fetch(n))
        ypart[order[n]] = product(n)

    def along_x(source, target, n, it, x):
        return pltpu.make_async_remote_copy(
            src_ref=source, dst_ref=target, send_sem=send_sem.at[n], recv_sem=recv_sem.at[it, n],
            device_id=(me, x), device_id_type=MESH,
        )

    def accumulate(it, some):
        stacked = [split(yfull[it, h]) for h in some]
        for b in range(columns // 256):
            at = pl.ds(b * 256, 256)
            pair = None
            for a, h in zip(stacked, some):
                one = lax.dot_general(a, high[h, :, at], NN, preferred_element_type=F32)
                one += lax.dot_general(a, low[h, :, at], NN, preferred_element_type=F32)
                pair = one if pair is None else pair + one
            zacc[:, at] += fold(pair)
        return stacked

    def peer_copy(ref, it, d, send, recv):
        return pltpu.make_async_remote_copy(
            src_ref=ref.at[it, mx], dst_ref=ref.at[it, mx], send_sem=send.at[d - 1], recv_sem=recv.at[it, d - 1],
            device_id=(me, lax.rem(mx + d, nx)), device_id_type=MESH,
        )

    def space_copy(source, ref, it, d, send, recv):
        s = lax.rem(me + d, ns)
        return pltpu.make_async_remote_copy(
            src_ref=source(s), dst_ref=ref.at[it, me], send_sem=send, recv_sem=recv.at[it],
            device_id=(s, mx), device_id_type=MESH,
        )

    def start_space(source, ref, it, send, recv):
        def go(d, carry):
            space_copy(source, ref, it, d, send, recv).start()
            return carry

        lax.fori_loop(1, ns, go, 0)

    def all_but_one(ref, it, sem):
        some = ref.at[it, pl.ds(0, ns - 1)]
        pltpu.make_async_copy(some, some, sem).wait()

    def sum_of(ref, it, count):
        total = ref[it, 0]
        for x in range(1, count):
            total = total + ref[it, x]
        return total

    def iteration(it, carry):
        far_copies, plain_copies, merged_copies = [], [], []
        for n, h in enumerate(far):
            k, side = divmod(n, 2)
            compute(it, n)
            copy = along_x(ypart.at[h], first_in.at[it, side, k], n, it, left if side else right)
            copy.start()
            far_copies.append(copy)
        for m, h in enumerate(plain):
            k, side = divmod(m, 2)
            n = len(far) + m
            compute(it, n)
            slot = second_in.at[it, side, k if side else k + third]
            copy = along_x(ypart.at[h], slot, n, it, left if side else right)
            copy.start()
            plain_copies.append(copy)
        for m, h in enumerate(merged):
            k, side = divmod(m, 2)
            n = len(far) + len(plain) + m
            compute(it, n)
            far_copies[m].wait_recv()
            ypart[h] += first_in[it, side, k]
            slot = second_in.at[it, side, k + third if side else k]
            copy = along_x(ypart.at[h], slot, n, it, left if side else right)
            copy.start()
            merged_copies.append(copy)

        base = pieces - len(own)

        @pl.when(it == 0)
        def _():
            for m in range(len(own)):
                fetch(base + m)

        @pl.when(it > 0)
        def _():
            for d in range(1, nx):
                peer_copy(gram_in, it, d, gram_send, gram_recv).wait()

        factor = inverse_factor(unpack(sum_of(gram_in, it, nx)))
        for m, h in enumerate(own):
            ypart[h] = product(base + m)
        factor_z[...] = factor

        spread = []

        def send_own(h, n, x):
            copy = along_x(yfull.at[it, h], yfull.at[it, h], n, it, x)
            copy.start()
            spread.append(copy)
            return copy

        straight = []
        for m, h in enumerate(own):
            k, side = divmod(m, 2)
            piece = k + side * third
            merged_copies[2 * k + side].wait_recv()
            plain_copies[2 * k + 1 - side].wait_recv()
            value = ypart[h] + second_in[it, 0, piece] + second_in[it, 1, piece]
            yfull[it, h] = exact(factor_z[...], value)
            straight.append(send_own(h, 18 + m, left if side else right))
        turned = []
        for m, h in enumerate(own):
            turned.append(send_own(h, 24 + m, right if m % 2 else left))

        zacc[...] = jnp.zeros_like(zacc)
        stacked = accumulate(it, own)
        gram = sum(gram_of(a) for a in stacked)
        own_in[it, mx] = pack(gram)
        for d in range(1, nx):
            peer_copy(own_in, it, d, own_send, own_recv).start()
        onward = []
        for k in steps:
            straight[2 * k].wait_recv()
            onward.append(send_own(part(left, k), 30 + 2 * k, right))
            straight[2 * k + 1].wait_recv()
            onward.append(send_own(part(right, k + third), 31 + 2 * k, left))
            accumulate(it, [part(left, k), part(right, k + third)])

        for d in range(1, nx):
            peer_copy(own_in, it, d, own_send, own_recv).wait()
        space_in[it, me] = sum_of(own_in, it, nx)
        start_space(lambda s: space_in.at[it, me], space_in, it, space_send, space_recv)

        for k in steps:
            turned[2 * k].wait_recv()
            turned[2 * k + 1].wait_recv()
            accumulate(it, [part(right, k), part(left, k + third)])
        for k in steps:
            onward[2 * k].wait_recv()
            onward[2 * k + 1].wait_recv()
            accumulate(it, [part(across, k), part(across, k + third)])

        for g in range(columns // 128):
            block = zacc[:, pl.ds(g * 128, 128)].reshape(4, 8, 128)
            for t in range(4):
                tiles_out[(g * 4 + t) // per, (g * 4 + t) % per] = block[t]
        start_space(lambda s: tiles_out.at[s], tiles_in, it, tile_send, tile_recv)
        tiles_in[it, me] = tiles_out[me]

        all_but_one(space_in, it, space_recv.at[it])
        factor_y[...] = inverse_factor(unpack(sum_of(space_in, it, ns)))
        all_but_one(space_in, it, space_send)
        for copy in far_copies + plain_copies + merged_copies + spread:
            copy.wait_send()

        all_but_one(tiles_in, it, tile_recv.at[it])
        sums[it, me] = sum_of(tiles_in, it, ns)
        start_space(lambda s: sums.at[it, me], sums, it, sum_send, sum_recv)
        all_but_one(tiles_in, it, tile_send)
        all_but_one(sums, it, sum_recv.at[it])
        gathered = sums[it].reshape(R, 8, 128)
        for g in range(columns // 128):
            block = gathered[g * 4 : g * 4 + 4].reshape(R, 128)
            zfull[:, g * 128 : g * 128 + 128] = exact(factor_y[...], block)

        @pl.when(it < ITERS)
        def _():
            stacked = split(zfull[...])
            zst[...] = stacked
            gram_in[it + 1, mx] = pack(gram_of(stacked))
            for d in range(1, nx):
                peer_copy(gram_in, it + 1, d, gram_send, gram_recv).start()

        all_but_one(sums, it, sum_send)
        return carry

    lax.fori_loop(0, ITERS + 1, iteration, 0)

    slices = columns // MODES
    zfull[...] = zfull[...] * (1.0 / math.sqrt(total_rows))
    sketched, rest = [], jnp.zeros((R, MODES), F32)
    for i in range(slices):
        block = zfull[:, pl.ds(i * MODES, MODES)]
        one = exact(following[...], block, NT)
        rest = rest + exact(one, block)
        sketched.append(one)
    sketched = jnp.concatenate(sketched, axis=1)
    last_out[:, pl.ds(0, MODES)] = rest
    last_out[:, pl.ds(MODES, 128)] = jnp.concatenate(
        [exact(sketched, sketched, NT), jnp.zeros((R, 128 - R), F32)], axis=1
    )
    last_in[mx] = last_out[...]

    def last_copy(d):
        return pltpu.make_async_remote_copy(
            src_ref=last_out, dst_ref=last_in.at[mx], send_sem=last_send.at[d - 1], recv_sem=last_recv.at[d - 1],
            device_id=(me, lax.rem(mx + d, nx)), device_id_type=MESH,
        )

    for d in range(1, nx):
        last_copy(d).start()

    def write(h):
        return pltpu.make_async_copy(
            ypart.at[h], basis_out.at[:, pl.ds(h * prows, prows)], out_sem.at[h]
        )

    for h in range(pieces):
        ypart[h] = exact(factor_y[...], yfull[ITERS, h]) * math.sqrt(total_rows)
        write(h).start()

    for d in range(1, nx):
        last_copy(d).wait()
    total = last_in[0]
    for x in range(1, nx):
        total = total + last_in[x]
    factor = inverse_factor(total[:, MODES : MODES + R])
    second_out[...] = exact(factor, sketched) * math.sqrt(unfold_rows)
    rest_out[...] = exact(factor, total[:, :MODES]) / math.sqrt(unfold_rows)
    for h in range(pieces):
        write(h).wait()


def solution(mesh):
    ns, nx = mesh.shape["space"], mesh.shape["param"]

    def shards(snapshots, sketch, following):
        rows, columns = snapshots.shape
        pieces = PIECES * nx
        prows = rows // pieces
        per = R // ns
        slices = columns // MODES
        steps = ITERS + 1
        dma = pltpu.SemaphoreType.DMA
        return pl.pallas_call(
            functools.partial(kernel, ns, nx, rows * ns, slices * R * nx),
            out_shape=(
                jax.ShapeDtypeStruct((R, rows), F32),
                jax.ShapeDtypeStruct((R, slices * R), F32),
                jax.ShapeDtypeStruct((R, MODES), F32),
            ),
            in_specs=[
                pl.BlockSpec(memory_space=pl.ANY),
                pl.BlockSpec(memory_space=pltpu.VMEM),
                pl.BlockSpec(memory_space=pltpu.VMEM),
            ],
            out_specs=(
                pl.BlockSpec(memory_space=pl.ANY),
                pl.BlockSpec(memory_space=pltpu.VMEM),
                pl.BlockSpec(memory_space=pltpu.VMEM),
            ),
            scratch_shapes=[
                pltpu.VMEM((pieces, prows, columns), BF16),
                pltpu.VMEM((pieces, prows, columns), BF16),
                pltpu.VMEM((4, prows, columns), F32),
                pltpu.VMEM((2 * R, columns), BF16),
                pltpu.VMEM((pieces, R, prows), F32),
                pltpu.VMEM((steps, 2, PIECES // 2, R, prows), F32),
                pltpu.VMEM((steps, 2, PIECES, R, prows), F32),
                pltpu.VMEM((steps, pieces, R, prows), F32),
                pltpu.VMEM((R, columns), F32),
                pltpu.VMEM((R, columns), F32),
                pltpu.VMEM((ns, per, 8, 128), F32),
                pltpu.VMEM((steps, ns, per, 8, 128), F32),
                pltpu.VMEM((steps, ns, per, 8, 128), F32),
                pltpu.VMEM((steps, nx, 8, 128), F32),
                pltpu.VMEM((steps, nx, 8, 128), F32),
                pltpu.VMEM((steps, ns, 8, 128), F32),
                pltpu.VMEM((R, MODES + 128), F32),
                pltpu.VMEM((nx, R, MODES + 128), F32),
                pltpu.VMEM((R, R), F32),
                pltpu.VMEM((R, R), F32),
                dma((4,)),
                dma((36,)),
                dma((steps, 36)),
                dma,
                dma((steps,)),
                dma,
                dma((steps,)),
                dma((nx - 1,)),
                dma((steps, nx - 1)),
                dma((nx - 1,)),
                dma((steps, nx - 1)),
                dma,
                dma((steps,)),
                dma((nx - 1,)),
                dma((nx - 1,)),
                dma((pieces,)),
            ],
            compiler_params=pltpu.CompilerParams(
                collective_id=0, has_side_effects=True, vmem_limit_bytes=60 * 1024 * 1024
            ),
        )(snapshots, sketch.T, following.T)

    return jax.shard_map(
        shards,
        mesh=mesh,
        in_specs=(P("space", "param"), P("param", None), P()),
        out_specs=(P(None, "space"), P(None, "param"), P()),
        check_vma=False,
    )
```

```python
import functools
import math

import jax
import jax.numpy as jnp
from jax import lax
from jax.experimental import pallas as pl
from jax.experimental.pallas import tpu as pltpu
from jax.sharding import PartitionSpec as P

MESH = pl.DeviceIdType.MESH
R = 32
MODES = 256
ITERS = 3
PIECES = 6
F32, BF16 = jnp.float32, jnp.bfloat16
NN = (((1,), (0,)), ((), ()))
NT = (((1,), (1,)), ((), ()))


def exact(a, b, dims=NN):
    return lax.dot_general(a, b, dims, precision=lax.Precision.HIGHEST, preferred_element_type=F32)


def split(value):
    high = value.astype(BF16)
    low = (value - high.astype(F32)).astype(BF16)
    return jnp.concatenate([high, low], axis=0)


def fold(pair):
    return pair[:R] + pair[R:]


def gram_of(stacked):
    both = lax.dot_general(stacked, stacked, NT, preferred_element_type=F32)
    half = fold(both)
    return half[:, :R] + half[:, R:]


def inverse_factor(gram):
    rows = lax.broadcasted_iota(jnp.int32, (R, R), 0)
    columns = lax.broadcasted_iota(jnp.int32, (R, R), 1)
    eye = jnp.where(rows == columns, 1.0, 0.0).astype(F32)
    work = jnp.concatenate([gram, eye], axis=1)
    below = lax.broadcasted_iota(jnp.int32, (R, 2 * R), 0)
    for j in range(R - 1):
        row = work[j : j + 1, :]
        scaled = row / row[:, j : j + 1]
        work = work - jnp.where(below > j, work[:, j : j + 1], 0.0) * scaled
    diagonal = jnp.sum(jnp.where(rows == columns, work[:, :R], 0.0), axis=1, keepdims=True)
    return work[:, R:] / jnp.sqrt(diagonal)


def pack(square):
    return jnp.concatenate([square[8 * i : 8 * i + 8] for i in range(4)], axis=1)


def unpack(tile):
    return jnp.concatenate([tile[:, R * i : R * i + R] for i in range(4)], axis=0)


def kernel(
    ns, nx, total_rows, unfold_rows,
    snap, sketch, following, basis_out, second_out, rest_out,
    high, low, high_t, low_t, stage, zst, ypart, first_in, second_in, yfull, zacc, zfull,
    tiles_out, tiles_in, sums, gram_in, own_in, space_in, last_out, last_in,
    factor_y,
    load_sem, send_sem, recv_sem, tile_send, tile_recv, sum_send, sum_recv,
    gram_send, gram_recv, own_send, own_recv, space_send, space_recv, last_send, last_recv, out_sem,
):
    me, mx = lax.axis_index("space"), lax.axis_index("param")
    right, left, across = lax.rem(mx + 1, nx), lax.rem(mx + nx - 1, nx), lax.rem(mx + 2, nx)
    pieces, prows, columns = high.shape
    per = tiles_out.shape[1]
    third = PIECES // 2
    loads = stage.shape[0]

    def part(quarter, piece):
        return quarter * PIECES + piece

    steps = range(third)
    far = [part(across, k + side * third) for k in steps for side in (0, 1)]
    plain = [h for k in steps for h in (part(right, k + third), part(left, k))]
    merged = [h for k in steps for h in (part(right, k), part(left, k + third))]
    own = [part(mx, k + side * third) for k in steps for side in (0, 1)]
    order = far + plain + merged + own
    quarters = [across] * 6 + [right, left] * 6 + [mx] * 6
    sides = [0, 1] * third + [1, 0] * third + [0, 1] * third * 2
    places = [(quarters[n] * 2 + sides[n], n % 6 // 2) for n in range(4 * PIECES)]

    def load(n):
        return pltpu.make_async_copy(
            snap.at[pl.ds(pl.multiple_of(order[n] * prows, prows), prows), :],
            stage.at[n % loads], load_sem.at[n % loads],
        )

    for n in range(loads):
        load(n).start()

    barrier = pltpu.get_barrier_semaphore()

    def greet(d, carry):
        pl.semaphore_signal(barrier, inc=1, device_id=(lax.rem(me + d, ns), mx), device_id_type=MESH)
        return carry

    lax.fori_loop(1, ns, greet, 0)
    for d in range(1, nx):
        pl.semaphore_signal(barrier, inc=1, device_id=(me, lax.rem(mx + d, nx)), device_id_type=MESH)

    zst[...] = split(sketch[...])
    pl.semaphore_wait(barrier, ns - 1 + nx - 1)

    def fetch(n):
        load(n).wait()

        def cut(i, carry):
            at = pl.ds(pl.multiple_of(i * 16, 16), 16)
            value = stage[n % loads, at, :]
            top = value.astype(BF16)
            high[order[n], at, :] = top
            low[order[n], at, :] = (value - top.astype(F32)).astype(BF16)
            return carry

        lax.fori_loop(0, prows // 16, cut, 0)
        if n + loads < pieces:
            load(n + loads).start()

    def product(n, first):
        h = order[n]
        if first:
            pair = lax.dot_general(zst[...], high[h], NT, preferred_element_type=F32)
            pair += lax.dot_general(zst[...], low[h], NT, preferred_element_type=F32)
        else:
            side, k = places[n]
            at = pl.ds(k * prows, prows)
            pair = lax.dot_general(zst[...], high_t[side, :, at], NN, preferred_element_type=F32)
            pair += lax.dot_general(zst[...], low_t[side, :, at], NN, preferred_element_type=F32)
        return fold(pair)

    def turn(source, target):
        def one(i, carry):
            for b in range(columns // 256):
                at = pl.ds(b * 256, 256)
                rows = [source[i * third + k, :, at] for k in steps]
                target[i, at, :] = jnp.concatenate(rows, axis=0).T
            return carry

        lax.fori_loop(0, pieces // third, one, 0)

    def in_turn(numbers, first, ready):
        ahead = None
        for n in numbers:
            if first:
                fetch(n)
            value = product(n, first)
            if ahead is not None:
                ready(*ahead)
            ahead = (n, value)
        ready(*ahead)

    def along_x(source, target, n, it, x):
        return pltpu.make_async_remote_copy(
            src_ref=source, dst_ref=target, send_sem=send_sem.at[n], recv_sem=recv_sem.at[it, n],
            device_id=(me, x), device_id_type=MESH,
        )

    def accumulate(it, some):
        stacked = [split(yfull[it, h]) for h in some]
        for b in range(columns // 256):
            at = pl.ds(b * 256, 256)
            pair = None
            for a, h in zip(stacked, some):
                one = lax.dot_general(a, high[h, :, at], NN, preferred_element_type=F32)
                one += lax.dot_general(a, low[h, :, at], NN, preferred_element_type=F32)
                pair = one if pair is None else pair + one
            zacc[:, at] += fold(pair)
        return stacked

    def peer_copy(ref, it, d, send, recv):
        return pltpu.make_async_remote_copy(
            src_ref=ref.at[it, mx], dst_ref=ref.at[it, mx], send_sem=send.at[d - 1], recv_sem=recv.at[it, d - 1],
            device_id=(me, lax.rem(mx + d, nx)), device_id_type=MESH,
        )

    nc = 2
    nz = min(4, ns // nc)
    ny = ns // (nc * nz)
    myy, myz, myc = me // (nz * nc), me // nc % nz, me % nc
    hops = sorted(
        (-min(dy, ny - dy) - min(dz, nz - dz), dy, dz, dc)
        for dy in range(ny) for dz in range(nz) for dc in range(nc) if dy or dz or dc
    )
    others = [
        ((lax.rem(myy + dy, ny) * nz + lax.rem(myz + dz, nz)) * nc + lax.rem(myc + dc, nc)) for _, dy, dz, dc in hops
    ]

    def start_space(source, ref, it, send, recv):
        for s in others:
            pltpu.make_async_remote_copy(
                src_ref=source(s), dst_ref=ref.at[it, me], send_sem=send, recv_sem=recv.at[it],
                device_id=(s, mx), device_id_type=MESH,
            ).start()

    def all_but_one(ref, it, sem):
        some = ref.at[it, pl.ds(0, ns - 1)]
        pltpu.make_async_copy(some, some, sem).wait()

    def sum_of(ref, it, count):
        total = ref[it, 0]
        for x in range(1, count):
            total = total + ref[it, x]
        return total

    def iteration(it, first):
        now = it % 2
        far_copies, plain_copies, merged_copies = [], [], []

        def send_far(n, value):
            k, side = divmod(n, 2)
            ypart[order[n]] = value
            copy = along_x(ypart.at[order[n]], first_in.at[now, side, k], n, it, left if side else right)
            copy.start()
            far_copies.append(copy)

        def send_plain(n, value):
            k, side = divmod(n - len(far), 2)
            ypart[order[n]] = value
            slot = second_in.at[now, side, k if side else k + third]
            copy = along_x(ypart.at[order[n]], slot, n, it, left if side else right)
            copy.start()
            plain_copies.append(copy)

        def send(n, value):
            (send_far if n < len(far) else send_plain)(n, value)

        def keep(n, value):
            ypart[order[n]] = value

        begun, base = len(far) + len(plain), pieces - len(own)
        in_turn(range(begun), first, send)
        in_turn(range(begun, base), first, keep)
        for m, h in enumerate(merged):
            k, side = divmod(m, 2)
            far_copies[m].wait_recv()
            ypart[h] += first_in[now, side, k]
            slot = second_in.at[now, side, k + third if side else k]
            copy = along_x(ypart.at[h], slot, begun + m, it, left if side else right)
            copy.start()
            merged_copies.append(copy)

        if first:
            factor = None
        else:
            for d in range(1, nx):
                peer_copy(gram_in, it, d, gram_send, gram_recv).wait()
            factor = inverse_factor(unpack(sum_of(gram_in, it, nx)))
        in_turn(range(base, pieces), first, keep)

        spread = []

        def send_own(h, n, x):
            copy = along_x(yfull.at[now, h], yfull.at[now, h], n, it, x)
            copy.start()
            spread.append(copy)
            return copy

        for copy in merged_copies + plain_copies:
            copy.wait_recv()
        value = jnp.concatenate(
            [
                ypart[h] + second_in[now, 0, m // 2 + m % 2 * third] + second_in[now, 1, m // 2 + m % 2 * third]
                for m, h in enumerate(own)
            ],
            axis=1,
        )
        if factor is not None:
            value = exact(factor, value)
        for m, h in enumerate(own):
            yfull[now, h] = value[:, m * prows : (m + 1) * prows]
        straight = [send_own(h, 18 + m, left if m % 2 else right) for m, h in enumerate(own)]
        turned = [send_own(h, 24 + m, right if m % 2 else left) for m, h in enumerate(own)]

        zacc[...] = jnp.zeros_like(zacc)
        accumulate(now, own)
        own_in[it, mx] = pack(gram_of(split(value)))
        for d in range(1, nx):
            peer_copy(own_in, it, d, own_send, own_recv).start()
        onward = []
        for k in steps:
            straight[2 * k].wait_recv()
            onward.append(send_own(part(left, k), 30 + 2 * k, right))
            straight[2 * k + 1].wait_recv()
            onward.append(send_own(part(right, k + third), 31 + 2 * k, left))
        accumulate(now, [h for k in steps for h in (part(left, k), part(right, k + third))])

        for d in range(1, nx):
            peer_copy(own_in, it, d, own_send, own_recv).wait()
        space_in[it, me] = sum_of(own_in, it, nx)
        start_space(lambda s: space_in.at[it, me], space_in, it, space_send, space_recv)

        for copy in turned:
            copy.wait_recv()
        accumulate(now, [h for k in steps for h in (part(right, k), part(left, k + third))])
        for some in (range(third - 1), range(third - 1, third)):
            for k in some:
                onward[2 * k].wait_recv()
                onward[2 * k + 1].wait_recv()
            accumulate(now, [h for k in some for h in (part(across, k), part(across, k + third))])

        for g in range(columns // 128):
            block = zacc[:, pl.ds(g * 128, 128)].reshape(4, 8, 128)
            for t in range(4):
                tiles_out[(g * 4 + t) // per, (g * 4 + t) % per] = block[t]
        start_space(lambda s: tiles_out.at[s], tiles_in, it, tile_send, tile_recv)
        tiles_in[it, me] = tiles_out[me]

        if first:
            turn(high, high_t)
        all_but_one(space_in, it, space_recv.at[it])
        factor_y[...] = inverse_factor(unpack(sum_of(space_in, it, ns)))
        all_but_one(space_in, it, space_send)
        for copy in far_copies + plain_copies + merged_copies + spread:
            copy.wait_send()

        all_but_one(tiles_in, it, tile_recv.at[it])
        sums[it, me] = sum_of(tiles_in, it, ns)
        start_space(lambda s: sums.at[it, me], sums, it, sum_send, sum_recv)
        all_but_one(tiles_in, it, tile_send)
        if first:
            turn(low, low_t)
        all_but_one(sums, it, sum_recv.at[it])
        gathered = sums[it].reshape(R, 8, 128)
        for g in range(columns // 128):
            block = gathered[g * 4 : g * 4 + 4].reshape(R, 128)
            zfull[:, g * 128 : g * 128 + 128] = exact(factor_y[...], block)

        def framed():
            stacked = split(zfull[...])
            zst[...] = stacked
            gram_in[it + 1, mx] = pack(gram_of(stacked))
            for d in range(1, nx):
                peer_copy(gram_in, it + 1, d, gram_send, gram_recv).start()

        if first:
            framed()
        else:
            pl.when(it < ITERS)(framed)
        all_but_one(sums, it, sum_send)

    iteration(0, True)

    def later(it, carry):
        iteration(it, False)
        return carry

    lax.fori_loop(1, ITERS + 1, later, 0)

    slices = columns // MODES
    zfull[...] = zfull[...] * (1.0 / math.sqrt(total_rows))
    sketched, rest = [], jnp.zeros((R, MODES), F32)
    for i in range(slices):
        block = zfull[:, pl.ds(i * MODES, MODES)]
        one = exact(following[...], block, NT)
        rest = rest + exact(one, block)
        sketched.append(one)
    sketched = jnp.concatenate(sketched, axis=1)
    last_out[:, pl.ds(0, MODES)] = rest
    last_out[:, pl.ds(MODES, 128)] = jnp.concatenate(
        [exact(sketched, sketched, NT), jnp.zeros((R, 128 - R), F32)], axis=1
    )
    last_in[mx] = last_out[...]

    def last_copy(d):
        return pltpu.make_async_remote_copy(
            src_ref=last_out, dst_ref=last_in.at[mx], send_sem=last_send.at[d - 1], recv_sem=last_recv.at[d - 1],
            device_id=(me, lax.rem(mx + d, nx)), device_id_type=MESH,
        )

    for d in range(1, nx):
        last_copy(d).start()

    def write(h):
        return pltpu.make_async_copy(
            ypart.at[h], basis_out.at[:, pl.ds(h * prows, prows)], out_sem.at[h]
        )

    for h in range(pieces):
        ypart[h] = exact(factor_y[...], yfull[ITERS % 2, h]) * math.sqrt(total_rows)
        write(h).start()

    for d in range(1, nx):
        last_copy(d).wait()
    total = last_in[0]
    for x in range(1, nx):
        total = total + last_in[x]
    factor = inverse_factor(total[:, MODES : MODES + R])
    second_out[...] = exact(factor, sketched) * math.sqrt(unfold_rows)
    rest_out[...] = exact(factor, total[:, :MODES]) / math.sqrt(unfold_rows)
    for h in range(pieces):
        write(h).wait()


def solution(mesh):
    ns, nx = mesh.shape["space"], mesh.shape["param"]

    def shards(snapshots, sketch, following):
        rows, columns = snapshots.shape
        pieces = PIECES * nx
        prows = rows // pieces
        per = R // ns
        slices = columns // MODES
        steps = ITERS + 1
        dma = pltpu.SemaphoreType.DMA
        return pl.pallas_call(
            functools.partial(kernel, ns, nx, rows * ns, slices * R * nx),
            out_shape=(
                jax.ShapeDtypeStruct((R, rows), F32),
                jax.ShapeDtypeStruct((R, slices * R), F32),
                jax.ShapeDtypeStruct((R, MODES), F32),
            ),
            in_specs=[
                pl.BlockSpec(memory_space=pl.ANY),
                pl.BlockSpec(memory_space=pltpu.VMEM),
                pl.BlockSpec(memory_space=pltpu.VMEM),
            ],
            out_specs=(
                pl.BlockSpec(memory_space=pl.ANY),
                pl.BlockSpec(memory_space=pltpu.VMEM),
                pl.BlockSpec(memory_space=pltpu.VMEM),
            ),
            scratch_shapes=[
                pltpu.VMEM((pieces, prows, columns), BF16),
                pltpu.VMEM((pieces, prows, columns), BF16),
                pltpu.VMEM((2 * nx, columns, rows // (2 * nx)), BF16),
                pltpu.VMEM((2 * nx, columns, rows // (2 * nx)), BF16),
                pltpu.VMEM((2, prows, columns), F32),
                pltpu.VMEM((2 * R, columns), BF16),
                pltpu.VMEM((pieces, R, prows), F32),
                pltpu.VMEM((2, 2, PIECES // 2, R, prows), F32),
                pltpu.VMEM((2, 2, PIECES, R, prows), F32),
                pltpu.VMEM((2, pieces, R, prows), F32),
                pltpu.VMEM((R, columns), F32),
                pltpu.VMEM((R, columns), F32),
                pltpu.VMEM((ns, per, 8, 128), F32),
                pltpu.VMEM((steps, ns, per, 8, 128), F32),
                pltpu.VMEM((steps, ns, per, 8, 128), F32),
                pltpu.VMEM((steps, nx, 8, 128), F32),
                pltpu.VMEM((steps, nx, 8, 128), F32),
                pltpu.VMEM((steps, ns, 8, 128), F32),
                pltpu.VMEM((R, MODES + 128), F32),
                pltpu.VMEM((nx, R, MODES + 128), F32),
                pltpu.VMEM((R, R), F32),
                dma((2,)),
                dma((36,)),
                dma((steps, 36)),
                dma,
                dma((steps,)),
                dma,
                dma((steps,)),
                dma((nx - 1,)),
                dma((steps, nx - 1)),
                dma((nx - 1,)),
                dma((steps, nx - 1)),
                dma,
                dma((steps,)),
                dma((nx - 1,)),
                dma((nx - 1,)),
                dma((pieces,)),
            ],
            compiler_params=pltpu.CompilerParams(
                collective_id=0, has_side_effects=True, vmem_limit_bytes=60 * 1024 * 1024
            ),
        )(snapshots, sketch.T, following.T)

    return jax.shard_map(
        shards,
        mesh=mesh,
        in_specs=(P("space", "param"), P("param", None), P()),
        out_specs=(P(None, "space"), P(None, "param"), P()),
        check_vma=False,
    )
```

```python
import functools
import math

import jax
import jax.numpy as jnp
from jax import lax
from jax.experimental import pallas as pl
from jax.experimental.pallas import tpu as pltpu
from jax.sharding import PartitionSpec as P

MESH = pl.DeviceIdType.MESH
R = 32
MODES = 256
ITERS = 3
PIECES = 6
F32, BF16 = jnp.float32, jnp.bfloat16
NN = (((1,), (0,)), ((), ()))
NT = (((1,), (1,)), ((), ()))


def exact(a, b, dims=NN):
    return lax.dot_general(a, b, dims, precision=lax.Precision.HIGHEST, preferred_element_type=F32)


def split(value):
    high = value.astype(BF16)
    low = (value - high.astype(F32)).astype(BF16)
    return jnp.concatenate([high, low], axis=0)


def fold(pair):
    return pair[:R] + pair[R:]


def gram_of(stacked):
    both = lax.dot_general(stacked, stacked, NT, preferred_element_type=F32)
    half = fold(both)
    return half[:, :R] + half[:, R:]


def inverse_factor(gram):
    rows = lax.broadcasted_iota(jnp.int32, (R, R), 0)
    columns = lax.broadcasted_iota(jnp.int32, (R, R), 1)
    eye = jnp.where(rows == columns, 1.0, 0.0).astype(F32)
    work = jnp.concatenate([gram, eye], axis=1)
    below = lax.broadcasted_iota(jnp.int32, (R, 2 * R), 0)
    for j in range(R - 1):
        row = work[j : j + 1, :]
        scaled = row / row[:, j : j + 1]
        work = work - jnp.where(below > j, work[:, j : j + 1], 0.0) * scaled
    diagonal = jnp.sum(jnp.where(rows == columns, work[:, :R], 0.0), axis=1, keepdims=True)
    return work[:, R:] / jnp.sqrt(diagonal)


def pack(square):
    return jnp.concatenate([square[8 * i : 8 * i + 8] for i in range(4)], axis=1)


def unpack(tile):
    return jnp.concatenate([tile[:, R * i : R * i + R] for i in range(4)], axis=0)


def kernel(
    ns, nx, total_rows, unfold_rows,
    snap, sketch, following, basis_out, second_out, rest_out,
    high, low, high_t, low_t, stage, zst, ypart, first_in, second_in, yfull, zacc, zfull,
    tiles_out, tiles_in, sums, gram_in, own_in, space_in, last_out, last_in,
    factor_y,
    load_sem, send_sem, recv_sem, tile_send, tile_recv, sum_send, sum_recv,
    gram_send, gram_recv, own_send, own_recv, space_send, space_recv, last_send, last_recv, out_sem,
):
    me, mx = lax.axis_index("space"), lax.axis_index("param")
    right, left, across = lax.rem(mx + 1, nx), lax.rem(mx + nx - 1, nx), lax.rem(mx + 2, nx)
    pieces, prows, columns = high.shape
    per = tiles_out.shape[1]
    third = PIECES // 2
    loads = stage.shape[0]

    def part(quarter, piece):
        return quarter * PIECES + piece

    steps = range(third)
    far = [part(across, k + side * third) for k in steps for side in (0, 1)]
    plain = [h for k in steps for h in (part(right, k + third), part(left, k))]
    merged = [h for k in steps for h in (part(right, k), part(left, k + third))]
    own = [part(mx, k + side * third) for k in steps for side in (0, 1)]
    order = far + plain + merged + own
    quarters = [across] * 6 + [right, left] * 6 + [mx] * 6
    sides = [0, 1] * third + [1, 0] * third + [0, 1] * third * 2
    places = [(quarters[n] * 2 + sides[n], n % 6 // 2) for n in range(4 * PIECES)]

    grouped = [base + 2 * k + side for base in range(0, 4 * PIECES, PIECES) for side in (0, 1) for k in steps]

    def load(i):
        return pltpu.make_async_copy(
            snap.at[pl.ds(pl.multiple_of(order[grouped[i]] * prows, prows), prows), :],
            stage.at[i % loads], load_sem.at[i % loads],
        )

    for n in range(loads):
        load(n).start()

    barrier = pltpu.get_barrier_semaphore()

    def greet(d, carry):
        pl.semaphore_signal(barrier, inc=1, device_id=(lax.rem(me + d, ns), mx), device_id_type=MESH)
        return carry

    lax.fori_loop(1, ns, greet, 0)
    for d in range(1, nx):
        pl.semaphore_signal(barrier, inc=1, device_id=(me, lax.rem(mx + d, nx)), device_id_type=MESH)

    zst[...] = split(sketch[...])

    def fetch(i):
        load(i).wait()
        n = grouped[i]

        def cut(row, carry):
            at = pl.ds(pl.multiple_of(row * 16, 16), 16)
            value = stage[i % loads, at, :]
            top = value.astype(BF16)
            high[order[n], at, :] = top
            low[order[n], at, :] = (value - top.astype(F32)).astype(BF16)
            return carry

        lax.fori_loop(0, prows // 16, cut, 0)
        if i + loads < pieces:
            load(i + loads).start()

    def product(n, first):
        h = order[n]
        if first:
            pair = lax.dot_general(zst[...], high[h], NT, preferred_element_type=F32)
            pair += lax.dot_general(zst[...], low[h], NT, preferred_element_type=F32)
        else:
            side, k = places[n]
            at = pl.ds(k * prows, prows)
            pair = lax.dot_general(zst[...], high_t[side, :, at], NN, preferred_element_type=F32)
            pair += lax.dot_general(zst[...], low_t[side, :, at], NN, preferred_element_type=F32)
        return fold(pair)

    def turn(source, target):
        def one(i, carry):
            for b in range(columns // 256):
                at = pl.ds(b * 256, 256)
                rows = [source[i * third + k, :, at] for k in steps]
                target[i, at, :] = jnp.concatenate(rows, axis=0).T
            return carry

        lax.fori_loop(0, pieces // third, one, 0)

    def in_turn(numbers, first, ready):
        if first:
            for at in range(numbers[0], numbers[-1] + 1, third):
                for i in range(at, at + third):
                    fetch(i)
                for n, value in [(grouped[i], product(grouped[i], True)) for i in range(at, at + third)]:
                    ready(n, value)
            return
        ahead = None
        for n in numbers:
            value = product(n, first)
            if ahead is not None:
                ready(*ahead)
            ahead = (n, value)
        ready(*ahead)

    def along_x(source, target, n, it, x):
        return pltpu.make_async_remote_copy(
            src_ref=source, dst_ref=target, send_sem=send_sem.at[n], recv_sem=recv_sem.at[it, n],
            device_id=(me, x), device_id_type=MESH,
        )

    def accumulate(it, some):
        stacked = [split(yfull[it, h]) for h in some]
        for b in range(columns // 256):
            at = pl.ds(b * 256, 256)
            pair = None
            for a, h in zip(stacked, some):
                one = lax.dot_general(a, high[h, :, at], NN, preferred_element_type=F32)
                one += lax.dot_general(a, low[h, :, at], NN, preferred_element_type=F32)
                pair = one if pair is None else pair + one
            zacc[:, at] += fold(pair)
        return stacked

    def peer_copy(ref, it, d, send, recv):
        return pltpu.make_async_remote_copy(
            src_ref=ref.at[it, mx], dst_ref=ref.at[it, mx], send_sem=send.at[d - 1], recv_sem=recv.at[it, d - 1],
            device_id=(me, lax.rem(mx + d, nx)), device_id_type=MESH,
        )

    nc = 2
    nz = min(4, ns // nc)
    ny = ns // (nc * nz)
    myy, myz, myc = me // (nz * nc), me // nc % nz, me % nc
    hops = sorted(
        (-min(dy, ny - dy) - min(dz, nz - dz), dy, dz, dc)
        for dy in range(ny) for dz in range(nz) for dc in range(nc) if dy or dz or dc
    )
    others = [
        ((lax.rem(myy + dy, ny) * nz + lax.rem(myz + dz, nz)) * nc + lax.rem(myc + dc, nc)) for _, dy, dz, dc in hops
    ]

    def start_space(source, ref, it, send, recv):
        for s in others:
            pltpu.make_async_remote_copy(
                src_ref=source(s), dst_ref=ref.at[it, me], send_sem=send, recv_sem=recv.at[it],
                device_id=(s, mx), device_id_type=MESH,
            ).start()

    def all_but_one(ref, it, sem):
        some = ref.at[it, pl.ds(0, ns - 1)]
        pltpu.make_async_copy(some, some, sem).wait()

    def sum_of(ref, it, count):
        total = ref[it, 0]
        for x in range(1, count):
            total = total + ref[it, x]
        return total

    def iteration(it, first):
        now = it % 2
        far_copies, plain_copies, merged_copies = {}, {}, []

        def send_far(n, value):
            k, side = divmod(n, 2)
            if first and not far_copies:
                pl.semaphore_wait(barrier, ns - 1 + nx - 1)
            ypart[order[n]] = value
            copy = along_x(ypart.at[order[n]], first_in.at[now, side, k], n, it, left if side else right)
            copy.start()
            far_copies[n] = copy

        def send_plain(n, value):
            k, side = divmod(n - len(far), 2)
            ypart[order[n]] = value
            slot = second_in.at[now, side, k if side else k + third]
            copy = along_x(ypart.at[order[n]], slot, n, it, left if side else right)
            copy.start()
            plain_copies[n - len(far)] = copy

        def keep(n, value):
            ypart[order[n]] = value

        begun, base = len(far) + len(plain), pieces - len(own)
        in_turn(range(len(far)), first, send_far)
        if not first:
            gram_in[it, mx] = pack(gram_of(zst[...]))
            for d in range(1, nx):
                peer_copy(gram_in, it, d, gram_send, gram_recv).start()
        in_turn(range(len(far), begun), first, send_plain)
        in_turn(range(begun, base), first, keep)
        for m, h in enumerate(merged):
            k, side = divmod(m, 2)
            far_copies[m].wait_recv()
            ypart[h] += first_in[now, side, k]
            slot = second_in.at[now, side, k + third if side else k]
            copy = along_x(ypart.at[h], slot, begun + m, it, left if side else right)
            copy.start()
            merged_copies.append(copy)

        if first:
            factor = None
        else:
            for d in range(1, nx):
                peer_copy(gram_in, it, d, gram_send, gram_recv).wait()
            factor = inverse_factor(unpack(sum_of(gram_in, it, nx)))
        in_turn(range(base, pieces), first, keep)

        spread = []

        def send_own(h, n, x):
            copy = along_x(yfull.at[now, h], yfull.at[now, h], n, it, x)
            copy.start()
            spread.append(copy)
            return copy

        straight, turned, values = [], [], []

        def cross(k):
            for m in (2 * k, 2 * k + 1):
                turned.append(send_own(own[m], 24 + m, right if m % 2 else left))

        for k in steps:
            value = []
            for m in (2 * k, 2 * k + 1):
                merged_copies[m].wait_recv()
                plain_copies[m].wait_recv()
            for m in (2 * k, 2 * k + 1):
                piece = k + m % 2 * third
                value.append(ypart[own[m]] + second_in[now, 0, piece] + second_in[now, 1, piece])
            value = jnp.concatenate(value, axis=1)
            if factor is not None:
                value = exact(factor, value)
            values.append(value)
            for m in (2 * k, 2 * k + 1):
                yfull[now, own[m]] = value[:, m % 2 * prows : (m % 2 + 1) * prows]
                straight.append(send_own(own[m], 18 + m, left if m % 2 else right))
            if k > 0:
                cross(k - 1)
        cross(third - 1)

        zacc[...] = jnp.zeros_like(zacc)
        accumulate(now, own)
        own_in[it, mx] = pack(gram_of(split(jnp.concatenate(values, axis=1))))
        for d in range(1, nx):
            peer_copy(own_in, it, d, own_send, own_recv).start()
        onward = []
        for k in steps:
            straight[2 * k].wait_recv()
            onward.append(send_own(part(left, k), 30 + 2 * k, right))
            straight[2 * k + 1].wait_recv()
            onward.append(send_own(part(right, k + third), 31 + 2 * k, left))
        accumulate(now, [h for k in steps for h in (part(left, k), part(right, k + third))])

        for d in range(1, nx):
            peer_copy(own_in, it, d, own_send, own_recv).wait()
        space_in[it, me] = sum_of(own_in, it, nx)
        start_space(lambda s: space_in.at[it, me], space_in, it, space_send, space_recv)

        for copy in turned:
            copy.wait_recv()
        accumulate(now, [h for k in steps for h in (part(right, k), part(left, k + third))])
        for some in (range(third - 1), range(third - 1, third)):
            for k in some:
                onward[2 * k].wait_recv()
                onward[2 * k + 1].wait_recv()
            accumulate(now, [h for k in some for h in (part(across, k), part(across, k + third))])

        for g in range(columns // 128):
            block = zacc[:, pl.ds(g * 128, 128)].reshape(4, 8, 128)
            for t in range(4):
                tiles_out[(g * 4 + t) // per, (g * 4 + t) % per] = block[t]
        start_space(lambda s: tiles_out.at[s], tiles_in, it, tile_send, tile_recv)
        tiles_in[it, me] = tiles_out[me]

        if first:
            turn(high, high_t)
        all_but_one(space_in, it, space_recv.at[it])
        factor_y[...] = inverse_factor(unpack(sum_of(space_in, it, ns)))
        all_but_one(space_in, it, space_send)
        for copy in [*far_copies.values(), *plain_copies.values(), *merged_copies, *spread]:
            copy.wait_send()

        all_but_one(tiles_in, it, tile_recv.at[it])
        sums[it, me] = sum_of(tiles_in, it, ns)
        start_space(lambda s: sums.at[it, me], sums, it, sum_send, sum_recv)
        all_but_one(tiles_in, it, tile_send)
        if first:
            turn(low, low_t)
        all_but_one(sums, it, sum_recv.at[it])
        gathered = sums[it].reshape(R, 8, 128)
        for g in range(columns // 128):
            block = gathered[g * 4 : g * 4 + 4].reshape(R, 128)
            zfull[:, g * 128 : g * 128 + 128] = exact(factor_y[...], block)

        zst[...] = split(zfull[...])
        all_but_one(sums, it, sum_send)

    iteration(0, True)

    def later(it, carry):
        iteration(it, False)
        return carry

    lax.fori_loop(1, ITERS + 1, later, 0)

    slices = columns // MODES
    zfull[...] = zfull[...] * (1.0 / math.sqrt(total_rows))
    sketched, rest = [], jnp.zeros((R, MODES), F32)
    for i in range(slices):
        block = zfull[:, pl.ds(i * MODES, MODES)]
        one = exact(following[...], block, NT)
        rest = rest + exact(one, block)
        sketched.append(one)
    sketched = jnp.concatenate(sketched, axis=1)
    last_out[:, pl.ds(0, MODES)] = rest
    last_out[:, pl.ds(MODES, 128)] = jnp.concatenate(
        [exact(sketched, sketched, NT), jnp.zeros((R, 128 - R), F32)], axis=1
    )
    last_in[mx] = last_out[...]

    def last_copy(d):
        return pltpu.make_async_remote_copy(
            src_ref=last_out, dst_ref=last_in.at[mx], send_sem=last_send.at[d - 1], recv_sem=last_recv.at[d - 1],
            device_id=(me, lax.rem(mx + d, nx)), device_id_type=MESH,
        )

    for d in range(1, nx):
        last_copy(d).start()

    def write(h):
        return pltpu.make_async_copy(
            ypart.at[h], basis_out.at[:, pl.ds(h * prows, prows)], out_sem.at[h]
        )

    for q in range(nx):
        some = range(q * PIECES, (q + 1) * PIECES)
        value = jnp.concatenate([yfull[ITERS % 2, h] for h in some], axis=1)
        value = exact(factor_y[...], value) * math.sqrt(total_rows)
        for h in some:
            ypart[h] = value[:, h % PIECES * prows : (h % PIECES + 1) * prows]
            write(h).start()

    for d in range(1, nx):
        last_copy(d).wait()
    total = last_in[0]
    for x in range(1, nx):
        total = total + last_in[x]
    factor = inverse_factor(total[:, MODES : MODES + R])
    second_out[...] = exact(factor, sketched) * math.sqrt(unfold_rows)
    rest_out[...] = exact(factor, total[:, :MODES]) / math.sqrt(unfold_rows)
    for h in range(pieces):
        write(h).wait()


def move(basis, second, rest, basis_out, second_out, rest_out, sem):
    pairs = ((basis, basis_out), (second, second_out), (rest, rest_out))
    copies = [pltpu.make_async_copy(a, b, sem.at[n]) for n, (a, b) in enumerate(pairs)]
    for copy in copies:
        copy.start()
    for copy in copies:
        copy.wait()


def solution(mesh):
    ns, nx = mesh.shape["space"], mesh.shape["param"]

    def shards(snapshots, sketch, following):
        rows, columns = snapshots.shape
        pieces = PIECES * nx
        prows = rows // pieces
        per = R // ns
        slices = columns // MODES
        steps = ITERS + 1
        dma = pltpu.SemaphoreType.DMA
        made = pl.pallas_call(
            functools.partial(kernel, ns, nx, rows * ns, slices * R * nx),
            out_shape=(
                jax.ShapeDtypeStruct((R, rows), F32),
                jax.ShapeDtypeStruct((R, slices * R), F32),
                jax.ShapeDtypeStruct((R, MODES), F32),
            ),
            in_specs=[
                pl.BlockSpec(memory_space=pl.ANY),
                pl.BlockSpec(memory_space=pltpu.VMEM),
                pl.BlockSpec(memory_space=pltpu.VMEM),
            ],
            out_specs=(
                pl.BlockSpec(memory_space=pl.ANY),
                pl.BlockSpec(memory_space=pltpu.VMEM),
                pl.BlockSpec(memory_space=pltpu.VMEM),
            ),
            scratch_shapes=[
                pltpu.VMEM((pieces, prows, columns), BF16),
                pltpu.VMEM((pieces, prows, columns), BF16),
                pltpu.VMEM((2 * nx, columns, rows // (2 * nx)), BF16),
                pltpu.VMEM((2 * nx, columns, rows // (2 * nx)), BF16),
                pltpu.VMEM((4, prows, columns), F32),
                pltpu.VMEM((2 * R, columns), BF16),
                pltpu.VMEM((pieces, R, prows), F32),
                pltpu.VMEM((2, 2, PIECES // 2, R, prows), F32),
                pltpu.VMEM((2, 2, PIECES, R, prows), F32),
                pltpu.VMEM((2, pieces, R, prows), F32),
                pltpu.VMEM((R, columns), F32),
                pltpu.VMEM((R, columns), F32),
                pltpu.VMEM((ns, per, 8, 128), F32),
                pltpu.VMEM((steps, ns, per, 8, 128), F32),
                pltpu.VMEM((steps, ns, per, 8, 128), F32),
                pltpu.VMEM((steps, nx, 8, 128), F32),
                pltpu.VMEM((steps, nx, 8, 128), F32),
                pltpu.VMEM((steps, ns, 8, 128), F32),
                pltpu.VMEM((R, MODES + 128), F32),
                pltpu.VMEM((nx, R, MODES + 128), F32),
                pltpu.VMEM((R, R), F32),
                dma((4,)),
                dma((36,)),
                dma((steps, 36)),
                dma,
                dma((steps,)),
                dma,
                dma((steps,)),
                dma((nx - 1,)),
                dma((steps, nx - 1)),
                dma((nx - 1,)),
                dma((steps, nx - 1)),
                dma,
                dma((steps,)),
                dma((nx - 1,)),
                dma((nx - 1,)),
                dma((pieces,)),
            ],
            compiler_params=pltpu.CompilerParams(
                collective_id=0, has_side_effects=True, vmem_limit_bytes=60 * 1024 * 1024
            ),
        )(snapshots, sketch.T, following.T)
        anywhere = pl.BlockSpec(memory_space=pl.ANY)
        return pl.pallas_call(
            move,
            out_shape=tuple(jax.ShapeDtypeStruct(one.shape, F32) for one in made),
            in_specs=[anywhere] * 3,
            out_specs=(anywhere,) * 3,
            scratch_shapes=[dma((3,))],
        )(*made)

    return jax.shard_map(
        shards,
        mesh=mesh,
        in_specs=(P("space", "param"), P("param", None), P()),
        out_specs=(P(None, "space"), P(None, "param"), P()),
        check_vma=False,
    )
```

```python
import functools
import math

import jax
import jax.numpy as jnp
from jax import lax
from jax.experimental import pallas as pl
from jax.experimental.pallas import tpu as pltpu
from jax.sharding import PartitionSpec as P

MESH = pl.DeviceIdType.MESH
R = 32
MOVES = 4
MODES = 256
ITERS = 3
BLOCK = 8
PIECES = 6
F32, BF16 = jnp.float32, jnp.bfloat16
NN = (((1,), (0,)), ((), ()))
NT = (((1,), (1,)), ((), ()))


def exact(a, b, dims=NN):
    return lax.dot_general(a, b, dims, precision=lax.Precision.HIGHEST, preferred_element_type=F32)


def split(value):
    high = value.astype(BF16)
    low = (value - high.astype(F32)).astype(BF16)
    return jnp.concatenate([high, low], axis=0)


def fold(pair):
    return pair[:R] + pair[R:]


def gram_of(stacked):
    both = lax.dot_general(stacked, stacked, NT, preferred_element_type=F32)
    half = fold(both)
    return half[:, :R] + half[:, R:]


def inverse_factor(gram):
    wide = (R, 2 * R)
    rows = lax.broadcasted_iota(jnp.int32, (R, R), 0)
    columns = lax.broadcasted_iota(jnp.int32, (R, R), 1)
    eye = jnp.where(rows == columns, 1.0, 0.0).astype(F32)
    work = jnp.concatenate([gram, eye], axis=1)
    below = lax.broadcasted_iota(jnp.int32, wide, 0)
    for j in range(0, R, BLOCK):
        row = [work[j + i : j + i + 1, :] for i in range(BLOCK)]
        spread = [[jnp.broadcast_to(row[i][:, j + k : j + k + 1], (1, 2 * R)) for k in range(BLOCK)] for i in range(BLOCK)]
        column = [jnp.broadcast_to(work[:, j + i : j + i + 1], wide) for i in range(BLOCK)]
        for i in range(BLOCK):
            if j + i == R - 1:
                break
            inverse = 1.0 / spread[i][i]
            scaled = row[i] * inverse
            work = work - jnp.where(below > j + i, column[i], 0.0) * scaled
            for k in range(i + 1, BLOCK):
                ratio = spread[i][k] * inverse
                row[k] = row[k] - spread[i][k] * scaled
                column[k] = column[k] - column[i] * ratio
                for m in range(k, BLOCK):
                    spread[k][m] = spread[k][m] - spread[i][m] * ratio
    diagonal = jnp.sum(jnp.where(rows == columns, work[:, :R], 0.0), axis=1, keepdims=True)
    return work[:, R:] / jnp.sqrt(diagonal)


def pack(square):
    return jnp.concatenate([square[8 * i : 8 * i + 8] for i in range(4)], axis=1)


def unpack(tile):
    return jnp.concatenate([tile[:, R * i : R * i + R] for i in range(4)], axis=0)


def kernel(
    ns, nx, total_rows, unfold_rows,
    snap, sketch, following, basis_out, second_out, rest_out,
    high, low, high_t, low_t, stage, zst, ypart, first_in, second_in, yfull, zacc, zfull,
    tiles_out, tiles_in, sums, gram_in, own_in, space_in, last_out, last_in,
    factor_y,
    load_sem, send_sem, recv_sem, tile_send, tile_recv, sum_send, sum_recv,
    gram_send, gram_recv, own_send, own_recv, space_send, space_recv, last_send, last_recv, out_sem,
):
    me, mx = lax.axis_index("space"), lax.axis_index("param")
    right, left, across = lax.rem(mx + 1, nx), lax.rem(mx + nx - 1, nx), lax.rem(mx + 2, nx)
    pieces, prows, columns = high.shape
    per = tiles_out.shape[1]
    third = PIECES // 2
    loads = stage.shape[0]

    def part(quarter, piece):
        return quarter * PIECES + piece

    steps = range(third)
    far = [part(across, k + side * third) for k in steps for side in (0, 1)]
    plain = [h for k in steps for h in (part(right, k + third), part(left, k))]
    merged = [h for k in steps for h in (part(right, k), part(left, k + third))]
    own = [part(mx, k + side * third) for k in steps for side in (0, 1)]
    order = far + plain + merged + own
    quarters = [across] * 6 + [right, left] * 6 + [mx] * 6
    sides = [0, 1] * third + [1, 0] * third + [0, 1] * third * 2
    places = [(quarters[n] * 2 + sides[n], n % 6 // 2) for n in range(4 * PIECES)]

    def load(n):
        return pltpu.make_async_copy(
            snap.at[pl.ds(pl.multiple_of(order[n] * prows, prows), prows), :],
            stage.at[n % loads], load_sem.at[n % loads],
        )

    for n in range(loads):
        load(n).start()

    barrier = pltpu.get_barrier_semaphore()

    def greet(d, carry):
        pl.semaphore_signal(barrier, inc=1, device_id=(lax.rem(me + d, ns), mx), device_id_type=MESH)
        return carry

    lax.fori_loop(1, ns, greet, 0)
    for d in range(1, nx):
        pl.semaphore_signal(barrier, inc=1, device_id=(me, lax.rem(mx + d, nx)), device_id_type=MESH)

    zst[...] = split(sketch[...])

    def product(n, first):
        h = order[n]
        if first:
            load(n).wait()
            value = stage[n % loads]
            top = value.astype(BF16)
            rest = (value - top.astype(F32)).astype(BF16)
            high[h] = top
            low[h] = rest
            pair = lax.dot_general(zst[...], top, NT, preferred_element_type=F32)
            pair += lax.dot_general(zst[...], rest, NT, preferred_element_type=F32)
            if n + loads < pieces:
                load(n + loads).start()
        else:
            side, k = places[n]
            at = pl.ds(k * prows, prows)
            pair = lax.dot_general(zst[...], high_t[side, :, at], NN, preferred_element_type=F32)
            pair += lax.dot_general(zst[...], low_t[side, :, at], NN, preferred_element_type=F32)
        return fold(pair)

    def turn(source, target):
        def one(i, carry):
            for b in range(columns // 256):
                at = pl.ds(b * 256, 256)
                rows = [source[i * third + k, :, at] for k in steps]
                target[i, at, :] = jnp.concatenate(rows, axis=0).T
            return carry

        lax.fori_loop(0, pieces // third, one, 0)

    def in_turn(numbers, first, ready):
        ahead = None
        for n in numbers:
            value = product(n, first)
            if ahead is not None:
                ready(*ahead)
            ahead = (n, value)
        ready(*ahead)

    def along_x(source, target, n, it, x):
        return pltpu.make_async_remote_copy(
            src_ref=source, dst_ref=target, send_sem=send_sem.at[n], recv_sem=recv_sem.at[it, n],
            device_id=(me, x), device_id_type=MESH,
        )

    def accumulate(it, some):
        stacked = [split(yfull[it, h]) for h in some]
        for b in range(columns // 256):
            at = pl.ds(b * 256, 256)
            pair = None
            for a, h in zip(stacked, some):
                one = lax.dot_general(a, high[h, :, at], NN, preferred_element_type=F32)
                one += lax.dot_general(a, low[h, :, at], NN, preferred_element_type=F32)
                pair = one if pair is None else pair + one
            zacc[:, at] += fold(pair)
        return stacked

    def peer_copy(ref, it, d, send, recv):
        return pltpu.make_async_remote_copy(
            src_ref=ref.at[it, mx], dst_ref=ref.at[it, mx], send_sem=send.at[d - 1], recv_sem=recv.at[it, d - 1],
            device_id=(me, lax.rem(mx + d, nx)), device_id_type=MESH,
        )

    nc = 2
    nz = min(4, ns // nc)
    ny = ns // (nc * nz)
    myy, myz, myc = me // (nz * nc), me // nc % nz, me % nc
    hops = sorted(
        (-min(dy, ny - dy) - min(dz, nz - dz), dy, dz, dc)
        for dy in range(ny) for dz in range(nz) for dc in range(nc) if dy or dz or dc
    )
    others = [
        ((lax.rem(myy + dy, ny) * nz + lax.rem(myz + dz, nz)) * nc + lax.rem(myc + dc, nc)) for _, dy, dz, dc in hops
    ]

    def start_space(source, ref, it, send, recv):
        for s in others:
            pltpu.make_async_remote_copy(
                src_ref=source(s), dst_ref=ref.at[it, me], send_sem=send, recv_sem=recv.at[it],
                device_id=(s, mx), device_id_type=MESH,
            ).start()

    def all_but_one(ref, it, sem):
        some = ref.at[it, pl.ds(0, ns - 1)]
        pltpu.make_async_copy(some, some, sem).wait()

    def sum_of(ref, it, count):
        total = ref[it, 0]
        for x in range(1, count):
            total = total + ref[it, x]
        return total

    def iteration(it, first):
        now = it % 2
        far_copies, plain_copies, merged_copies = {}, {}, []

        def send_far(n, value):
            k, side = divmod(n, 2)
            if first and not far_copies:
                pl.semaphore_wait(barrier, ns - 1 + nx - 1)
            ypart[order[n]] = value
            copy = along_x(ypart.at[order[n]], first_in.at[now, side, k], n, it, left if side else right)
            copy.start()
            far_copies[n] = copy

        def send_plain(n, value):
            k, side = divmod(n - len(far), 2)
            ypart[order[n]] = value
            slot = second_in.at[now, side, k if side else k + third]
            copy = along_x(ypart.at[order[n]], slot, n, it, left if side else right)
            copy.start()
            plain_copies[n - len(far)] = copy

        def keep(n, value):
            ypart[order[n]] = value

        begun, base = len(far) + len(plain), pieces - len(own)
        in_turn(range(len(far)), first, send_far)
        if not first:
            gram_in[it, mx] = pack(gram_of(zst[...]))
            for d in range(1, nx):
                peer_copy(gram_in, it, d, gram_send, gram_recv).start()
        in_turn(range(len(far), begun), first, send_plain)
        in_turn(range(begun, base), first, keep)
        for m, h in enumerate(merged):
            k, side = divmod(m, 2)
            far_copies[m].wait_recv()
            ypart[h] += first_in[now, side, k]
            slot = second_in.at[now, side, k + third if side else k]
            copy = along_x(ypart.at[h], slot, begun + m, it, left if side else right)
            copy.start()
            merged_copies.append(copy)

        if first:
            factor = None
        else:
            for d in range(1, nx):
                peer_copy(gram_in, it, d, gram_send, gram_recv).wait()
            factor = inverse_factor(unpack(sum_of(gram_in, it, nx)))
        in_turn(range(base, pieces), first, keep)

        spread = []

        def send_own(h, n, x):
            copy = along_x(yfull.at[now, h], yfull.at[now, h], n, it, x)
            copy.start()
            spread.append(copy)
            return copy

        straight, turned, values = [], [], []

        def cross(k):
            for m in (2 * k, 2 * k + 1):
                turned.append(send_own(own[m], 24 + m, right if m % 2 else left))

        for k in steps:
            value = []
            for m in (2 * k, 2 * k + 1):
                merged_copies[m].wait_recv()
                plain_copies[m].wait_recv()
            for m in (2 * k, 2 * k + 1):
                piece = k + m % 2 * third
                value.append(ypart[own[m]] + second_in[now, 0, piece] + second_in[now, 1, piece])
            value = jnp.concatenate(value, axis=1)
            if factor is not None:
                value = exact(factor, value)
            values.append(value)
            for m in (2 * k, 2 * k + 1):
                yfull[now, own[m]] = value[:, m % 2 * prows : (m % 2 + 1) * prows]
                straight.append(send_own(own[m], 18 + m, left if m % 2 else right))
            if k > 0:
                cross(k - 1)
        cross(third - 1)

        zacc[...] = jnp.zeros_like(zacc)
        accumulate(now, own)
        own_in[it, mx] = pack(gram_of(split(jnp.concatenate(values, axis=1))))
        for d in range(1, nx):
            peer_copy(own_in, it, d, own_send, own_recv).start()
        onward = []
        for k in steps:
            straight[2 * k].wait_recv()
            onward.append(send_own(part(left, k), 30 + 2 * k, right))
            straight[2 * k + 1].wait_recv()
            onward.append(send_own(part(right, k + third), 31 + 2 * k, left))
        accumulate(now, [h for k in steps for h in (part(left, k), part(right, k + third))])

        for d in range(1, nx):
            peer_copy(own_in, it, d, own_send, own_recv).wait()
        space_in[it, me] = sum_of(own_in, it, nx)
        start_space(lambda s: space_in.at[it, me], space_in, it, space_send, space_recv)

        for copy in turned:
            copy.wait_recv()
        accumulate(now, [h for k in steps for h in (part(right, k), part(left, k + third))])
        for some in (range(third - 1), range(third - 1, third)):
            for k in some:
                onward[2 * k].wait_recv()
                onward[2 * k + 1].wait_recv()
            accumulate(now, [h for k in some for h in (part(across, k), part(across, k + third))])

        for g in range(columns // 128):
            block = zacc[:, pl.ds(g * 128, 128)].reshape(4, 8, 128)
            for t in range(4):
                tiles_out[(g * 4 + t) // per, (g * 4 + t) % per] = block[t]
        start_space(lambda s: tiles_out.at[s], tiles_in, it, tile_send, tile_recv)
        tiles_in[it, me] = tiles_out[me]

        if first:
            turn(high, high_t)
        all_but_one(space_in, it, space_recv.at[it])
        factor_y[...] = inverse_factor(unpack(sum_of(space_in, it, ns)))
        all_but_one(space_in, it, space_send)
        for copy in [*far_copies.values(), *plain_copies.values(), *merged_copies, *spread]:
            copy.wait_send()

        all_but_one(tiles_in, it, tile_recv.at[it])
        sums[it, me] = sum_of(tiles_in, it, ns)
        start_space(lambda s: sums.at[it, me], sums, it, sum_send, sum_recv)
        all_but_one(tiles_in, it, tile_send)
        if first:
            turn(low, low_t)
        all_but_one(sums, it, sum_recv.at[it])
        gathered = sums[it].reshape(R, 8, 128)
        for g in range(columns // 128):
            block = gathered[g * 4 : g * 4 + 4].reshape(R, 128)
            zfull[:, g * 128 : g * 128 + 128] = exact(factor_y[...], block)

        zst[...] = split(zfull[...])
        all_but_one(sums, it, sum_send)

    iteration(0, True)

    def later(it, carry):
        iteration(it, False)
        return carry

    lax.fori_loop(1, ITERS + 1, later, 0)

    slices = columns // MODES
    zfull[...] = zfull[...] * (1.0 / math.sqrt(total_rows))
    sketched, rest = [], jnp.zeros((R, MODES), F32)
    for i in range(slices):
        block = zfull[:, pl.ds(i * MODES, MODES)]
        one = exact(following[...], block, NT)
        rest = rest + exact(one, block)
        sketched.append(one)
    sketched = jnp.concatenate(sketched, axis=1)
    last_out[:, pl.ds(0, MODES)] = rest
    last_out[:, pl.ds(MODES, 128)] = jnp.concatenate(
        [exact(sketched, sketched, NT), jnp.zeros((R, 128 - R), F32)], axis=1
    )
    last_in[mx] = last_out[...]

    def last_copy(d):
        return pltpu.make_async_remote_copy(
            src_ref=last_out, dst_ref=last_in.at[mx], send_sem=last_send.at[d - 1], recv_sem=last_recv.at[d - 1],
            device_id=(me, lax.rem(mx + d, nx)), device_id_type=MESH,
        )

    for d in range(1, nx):
        last_copy(d).start()

    def write(h):
        return pltpu.make_async_copy(
            ypart.at[h], basis_out.at[:, pl.ds(h * prows, prows)], out_sem.at[h]
        )

    for q in range(nx):
        some = range(q * PIECES, (q + 1) * PIECES)
        value = jnp.concatenate([yfull[ITERS % 2, h] for h in some], axis=1)
        value = exact(factor_y[...], value) * math.sqrt(total_rows)
        for h in some:
            ypart[h] = value[:, h % PIECES * prows : (h % PIECES + 1) * prows]
            write(h).start()

    for d in range(1, nx):
        last_copy(d).wait()
    total = last_in[0]
    for x in range(1, nx):
        total = total + last_in[x]
    factor = inverse_factor(total[:, MODES : MODES + R])
    second_out[...] = exact(factor, sketched) * math.sqrt(unfold_rows)
    rest_out[...] = exact(factor, total[:, :MODES]) / math.sqrt(unfold_rows)
    for h in range(pieces):
        write(h).wait()


def move(basis, second, rest, basis_out, second_out, rest_out, held, held_second, held_rest, sem, out_sem):
    width = basis.shape[1] // MOVES
    spans = [pl.ds(n * width, width) for n in range(MOVES)]
    ways = [(basis.at[:, at], held.at[:, at], basis_out.at[:, at]) for at in spans]
    ways += [(second, held_second, second_out), (rest, held_rest, rest_out)]
    ins = [pltpu.make_async_copy(a, b, sem.at[n]) for n, (a, b, c) in enumerate(ways)]
    outs = [pltpu.make_async_copy(b, c, out_sem.at[n]) for n, (a, b, c) in enumerate(ways)]
    for copy in ins:
        copy.start()
    for one, other in zip(ins, outs):
        one.wait()
        other.start()
    for copy in outs:
        copy.wait()


def solution(mesh):
    ns, nx = mesh.shape["space"], mesh.shape["param"]

    def shards(snapshots, sketch, following):
        rows, columns = snapshots.shape
        pieces = PIECES * nx
        prows = rows // pieces
        per = R // ns
        slices = columns // MODES
        steps = ITERS + 1
        dma = pltpu.SemaphoreType.DMA
        made = pl.pallas_call(
            functools.partial(kernel, ns, nx, rows * ns, slices * R * nx),
            out_shape=(
                jax.ShapeDtypeStruct((R, rows), F32),
                jax.ShapeDtypeStruct((R, slices * R), F32),
                jax.ShapeDtypeStruct((R, MODES), F32),
            ),
            in_specs=[
                pl.BlockSpec(memory_space=pl.ANY),
                pl.BlockSpec(memory_space=pltpu.VMEM),
                pl.BlockSpec(memory_space=pltpu.VMEM),
            ],
            out_specs=(
                pl.BlockSpec(memory_space=pl.ANY),
                pl.BlockSpec(memory_space=pltpu.VMEM),
                pl.BlockSpec(memory_space=pltpu.VMEM),
            ),
            scratch_shapes=[
                pltpu.VMEM((pieces, prows, columns), BF16),
                pltpu.VMEM((pieces, prows, columns), BF16),
                pltpu.VMEM((2 * nx, columns, rows // (2 * nx)), BF16),
                pltpu.VMEM((2 * nx, columns, rows // (2 * nx)), BF16),
                pltpu.VMEM((4, prows, columns), F32),
                pltpu.VMEM((2 * R, columns), BF16),
                pltpu.VMEM((pieces, R, prows), F32),
                pltpu.VMEM((2, 2, PIECES // 2, R, prows), F32),
                pltpu.VMEM((2, 2, PIECES, R, prows), F32),
                pltpu.VMEM((2, pieces, R, prows), F32),
                pltpu.VMEM((R, columns), F32),
                pltpu.VMEM((R, columns), F32),
                pltpu.VMEM((ns, per, 8, 128), F32),
                pltpu.VMEM((steps, ns, per, 8, 128), F32),
                pltpu.VMEM((steps, ns, per, 8, 128), F32),
                pltpu.VMEM((steps, nx, 8, 128), F32),
                pltpu.VMEM((steps, nx, 8, 128), F32),
                pltpu.VMEM((steps, ns, 8, 128), F32),
                pltpu.VMEM((R, MODES + 128), F32),
                pltpu.VMEM((nx, R, MODES + 128), F32),
                pltpu.VMEM((R, R), F32),
                dma((4,)),
                dma((36,)),
                dma((steps, 36)),
                dma,
                dma((steps,)),
                dma,
                dma((steps,)),
                dma((nx - 1,)),
                dma((steps, nx - 1)),
                dma((nx - 1,)),
                dma((steps, nx - 1)),
                dma,
                dma((steps,)),
                dma((nx - 1,)),
                dma((nx - 1,)),
                dma((pieces,)),
            ],
            compiler_params=pltpu.CompilerParams(
                collective_id=0, has_side_effects=True, vmem_limit_bytes=60 * 1024 * 1024
            ),
        )(snapshots, sketch.T, following.T)
        anywhere = pl.BlockSpec(memory_space=pl.ANY)
        return pl.pallas_call(
            move,
            out_shape=tuple(jax.ShapeDtypeStruct(one.shape, F32) for one in made),
            in_specs=[anywhere] * 3,
            out_specs=(anywhere,) * 3,
            scratch_shapes=[pltpu.VMEM(one.shape, F32) for one in made] + [dma((MOVES + 2,)), dma((MOVES + 2,))],
        )(*made)

    return jax.shard_map(
        shards,
        mesh=mesh,
        in_specs=(P("space", "param"), P("param", None), P()),
        out_specs=(P(None, "space"), P(None, "param"), P()),
        check_vma=False,
    )
```

```python
import functools
import math

import jax
import jax.numpy as jnp
from jax import lax
from jax.experimental import pallas as pl
from jax.experimental.pallas import tpu as pltpu
from jax.sharding import PartitionSpec as P

MESH = pl.DeviceIdType.MESH
R = 32
MOVES = 4
MODES = 256
ITERS = 3
BLOCK = 8
PIECES = 6
F32, BF16 = jnp.float32, jnp.bfloat16
NN = (((1,), (0,)), ((), ()))
NT = (((1,), (1,)), ((), ()))


def exact(a, b, dims=NN):
    return lax.dot_general(a, b, dims, precision=lax.Precision.HIGHEST, preferred_element_type=F32)


def split(value):
    high = value.astype(BF16)
    low = (value - high.astype(F32)).astype(BF16)
    return jnp.concatenate([high, low], axis=0)


def fold(pair):
    return pair[:R] + pair[R:]


def gram_of(stacked):
    both = lax.dot_general(stacked, stacked, NT, preferred_element_type=F32)
    half = fold(both)
    return half[:, :R] + half[:, R:]


def inverse_factor(gram):
    wide = (R, 2 * R)
    rows = lax.broadcasted_iota(jnp.int32, (R, R), 0)
    columns = lax.broadcasted_iota(jnp.int32, (R, R), 1)
    eye = jnp.where(rows == columns, 1.0, 0.0).astype(F32)
    work = jnp.concatenate([gram, eye], axis=1)
    below = lax.broadcasted_iota(jnp.int32, wide, 0)
    for j in range(0, R, BLOCK):
        row = [work[j + i : j + i + 1, :] for i in range(BLOCK)]
        spread = [[jnp.broadcast_to(row[i][:, j + k : j + k + 1], (1, 2 * R)) for k in range(BLOCK)] for i in range(BLOCK)]
        column = [jnp.broadcast_to(work[:, j + i : j + i + 1], wide) for i in range(BLOCK)]
        for i in range(BLOCK):
            if j + i == R - 1:
                break
            inverse = 1.0 / spread[i][i]
            scaled = row[i] * inverse
            work = work - jnp.where(below > j + i, column[i], 0.0) * scaled
            for k in range(i + 1, BLOCK):
                ratio = spread[i][k] * inverse
                row[k] = row[k] - spread[i][k] * scaled
                column[k] = column[k] - column[i] * ratio
                for m in range(k, BLOCK):
                    spread[k][m] = spread[k][m] - spread[i][m] * ratio
    diagonal = jnp.sum(jnp.where(rows == columns, work[:, :R], 0.0), axis=1, keepdims=True)
    return work[:, R:] / jnp.sqrt(diagonal)


def pack(square):
    return jnp.concatenate([square[8 * i : 8 * i + 8] for i in range(4)], axis=1)


def unpack(tile):
    return jnp.concatenate([tile[:, R * i : R * i + R] for i in range(4)], axis=0)


def kernel(
    ns, nx, total_rows, unfold_rows,
    snap, sketch_in, following_in, basis_out, second_out, rest_out,
    sketch, following, high, low, high_t, low_t, stage, zst, ypart, first_in, second_in, yfull, zacc, zfull,
    tiles_out, tiles_in, sums, gram_in, own_in, space_in, last_out, last_in,
    factor_y,
    small_sem, load_sem, send_sem, recv_sem, tile_send, tile_recv, sum_send, sum_recv,
    gram_send, gram_recv, own_send, own_recv, space_send, space_recv, last_send, last_recv, out_sem,
):
    me, mx = lax.axis_index("space"), lax.axis_index("param")
    right, left, across = lax.rem(mx + 1, nx), lax.rem(mx + nx - 1, nx), lax.rem(mx + 2, nx)
    pieces, prows, columns = high.shape
    per = tiles_out.shape[1]
    third = PIECES // 2
    loads = stage.shape[0]

    def part(quarter, piece):
        return quarter * PIECES + piece

    steps = range(third)
    far = [part(across, k + side * third) for k in steps for side in (0, 1)]
    plain = [h for k in steps for h in (part(right, k + third), part(left, k))]
    merged = [h for k in steps for h in (part(right, k), part(left, k + third))]
    own = [part(mx, k + side * third) for k in steps for side in (0, 1)]
    order = far + plain + merged + own
    quarters = [across] * 6 + [right, left] * 6 + [mx] * 6
    sides = [0, 1] * third + [1, 0] * third + [0, 1] * third * 2
    places = [(quarters[n] * 2 + sides[n], n % 6 // 2) for n in range(4 * PIECES)]

    def load(n):
        return pltpu.make_async_copy(
            snap.at[pl.ds(pl.multiple_of(order[n] * prows, prows), prows), :],
            stage.at[n % loads], load_sem.at[n % loads],
        )

    small = [
        pltpu.make_async_copy(sketch_in, sketch, small_sem.at[0]),
        pltpu.make_async_copy(following_in, following, small_sem.at[1]),
    ]
    small[0].start()
    for n in range(loads):
        load(n).start()
    small[1].start()

    barrier = pltpu.get_barrier_semaphore()

    def greet(d, carry):
        pl.semaphore_signal(barrier, inc=1, device_id=(lax.rem(me + d, ns), mx), device_id_type=MESH)
        return carry

    lax.fori_loop(1, ns, greet, 0)
    for d in range(1, nx):
        pl.semaphore_signal(barrier, inc=1, device_id=(me, lax.rem(mx + d, nx)), device_id_type=MESH)

    small[0].wait()
    zst[...] = split(sketch[...])

    def product(n, first):
        h = order[n]
        if first:
            load(n).wait()
            value = stage[n % loads]
            top = value.astype(BF16)
            rest = (value - top.astype(F32)).astype(BF16)
            high[h] = top
            low[h] = rest
            pair = lax.dot_general(zst[...], top, NT, preferred_element_type=F32)
            pair += lax.dot_general(zst[...], rest, NT, preferred_element_type=F32)
            if n + loads < pieces:
                load(n + loads).start()
        else:
            side, k = places[n]
            at = pl.ds(k * prows, prows)
            pair = lax.dot_general(zst[...], high_t[side, :, at], NN, preferred_element_type=F32)
            pair += lax.dot_general(zst[...], low_t[side, :, at], NN, preferred_element_type=F32)
        return fold(pair)

    def turn(source, target):
        def one(i, carry):
            for b in range(columns // 256):
                at = pl.ds(b * 256, 256)
                rows = [source[i * third + k, :, at] for k in steps]
                target[i, at, :] = jnp.concatenate(rows, axis=0).T
            return carry

        lax.fori_loop(0, pieces // third, one, 0)

    def in_turn(numbers, first, ready):
        ahead = None
        for n in numbers:
            value = product(n, first)
            if ahead is not None:
                ready(*ahead)
            ahead = (n, value)
        ready(*ahead)

    def along_x(source, target, n, it, x):
        return pltpu.make_async_remote_copy(
            src_ref=source, dst_ref=target, send_sem=send_sem.at[n], recv_sem=recv_sem.at[it, n],
            device_id=(me, x), device_id_type=MESH,
        )

    def accumulate(it, some):
        stacked = [split(yfull[it, h]) for h in some]
        for b in range(columns // 256):
            at = pl.ds(b * 256, 256)
            pair = None
            for a, h in zip(stacked, some):
                one = lax.dot_general(a, high[h, :, at], NN, preferred_element_type=F32)
                one += lax.dot_general(a, low[h, :, at], NN, preferred_element_type=F32)
                pair = one if pair is None else pair + one
            zacc[:, at] += fold(pair)
        return stacked

    def peer_copy(ref, it, d, send, recv):
        return pltpu.make_async_remote_copy(
            src_ref=ref.at[it, mx], dst_ref=ref.at[it, mx], send_sem=send.at[d - 1], recv_sem=recv.at[it, d - 1],
            device_id=(me, lax.rem(mx + d, nx)), device_id_type=MESH,
        )

    nc = 2
    nz = min(4, ns // nc)
    ny = ns // (nc * nz)
    myy, myz, myc = me // (nz * nc), me // nc % nz, me % nc
    hops = sorted(
        (-min(dy, ny - dy) - min(dz, nz - dz), dy, dz, dc)
        for dy in range(ny) for dz in range(nz) for dc in range(nc) if dy or dz or dc
    )
    others = [
        ((lax.rem(myy + dy, ny) * nz + lax.rem(myz + dz, nz)) * nc + lax.rem(myc + dc, nc)) for _, dy, dz, dc in hops
    ]

    def start_space(source, ref, it, send, recv):
        for s in others:
            pltpu.make_async_remote_copy(
                src_ref=source(s), dst_ref=ref.at[it, me], send_sem=send, recv_sem=recv.at[it],
                device_id=(s, mx), device_id_type=MESH,
            ).start()

    def all_but_one(ref, it, sem):
        some = ref.at[it, pl.ds(0, ns - 1)]
        pltpu.make_async_copy(some, some, sem).wait()

    def sum_of(ref, it, count):
        total = ref[it, 0]
        for x in range(1, count):
            total = total + ref[it, x]
        return total

    def iteration(it, first):
        now = it % 2
        far_copies, plain_copies, merged_copies = {}, {}, []

        def send_far(n, value):
            k, side = divmod(n, 2)
            if not first:
                ypart[order[n]] = value
            copy = along_x(ypart.at[order[n]], first_in.at[now, side, k], n, it, left if side else right)
            copy.start()
            far_copies[n] = copy

        def send_plain(n, value):
            k, side = divmod(n - len(far), 2)
            ypart[order[n]] = value
            slot = second_in.at[now, side, k if side else k + third]
            copy = along_x(ypart.at[order[n]], slot, n, it, left if side else right)
            copy.start()
            plain_copies[n - len(far)] = copy

        def keep(n, value):
            ypart[order[n]] = value

        begun, base = len(far) + len(plain), pieces - len(own)
        if first:
            in_turn(range(len(far)), first, keep)
            pl.semaphore_wait(barrier, ns - 1 + nx - 1)
            for n in range(len(far)):
                send_far(n, None)
        else:
            in_turn(range(len(far)), first, send_far)
            gram_in[it, mx] = pack(gram_of(zst[...]))
            for d in range(1, nx):
                peer_copy(gram_in, it, d, gram_send, gram_recv).start()
        in_turn(range(len(far), begun), first, send_plain)
        in_turn(range(begun, base), first, keep)
        for m, h in enumerate(merged):
            k, side = divmod(m, 2)
            far_copies[m].wait_recv()
            ypart[h] += first_in[now, side, k]
            slot = second_in.at[now, side, k + third if side else k]
            copy = along_x(ypart.at[h], slot, begun + m, it, left if side else right)
            copy.start()
            merged_copies.append(copy)

        if first:
            factor = None
        else:
            for d in range(1, nx):
                peer_copy(gram_in, it, d, gram_send, gram_recv).wait()
            factor = inverse_factor(unpack(sum_of(gram_in, it, nx)))
        in_turn(range(base, pieces), first, keep)

        spread = []

        def send_own(h, n, x):
            copy = along_x(yfull.at[now, h], yfull.at[now, h], n, it, x)
            copy.start()
            spread.append(copy)
            return copy

        straight, turned, values = [], [], []

        def cross(k):
            for m in (2 * k, 2 * k + 1):
                turned.append(send_own(own[m], 24 + m, right if m % 2 else left))

        for k in steps:
            value = []
            for m in (2 * k, 2 * k + 1):
                merged_copies[m].wait_recv()
                plain_copies[m].wait_recv()
            for m in (2 * k, 2 * k + 1):
                piece = k + m % 2 * third
                value.append(ypart[own[m]] + second_in[now, 0, piece] + second_in[now, 1, piece])
            value = jnp.concatenate(value, axis=1)
            if factor is not None:
                value = exact(factor, value)
            values.append(value)
            for m in (2 * k, 2 * k + 1):
                yfull[now, own[m]] = value[:, m % 2 * prows : (m % 2 + 1) * prows]
                straight.append(send_own(own[m], 18 + m, left if m % 2 else right))
            if 0 < k < third - 1:
                cross(k - 1)
        own_in[it, mx] = pack(gram_of(split(jnp.concatenate(values, axis=1))))
        for d in range(1, nx):
            peer_copy(own_in, it, d, own_send, own_recv).start()
        cross(third - 2)

        cross(third - 1)
        zacc[...] = jnp.zeros_like(zacc)
        accumulate(now, own)
        onward = []
        for k in steps:
            straight[2 * k].wait_recv()
            onward.append(send_own(part(left, k), 30 + 2 * k, right))
            straight[2 * k + 1].wait_recv()
            onward.append(send_own(part(right, k + third), 31 + 2 * k, left))
        accumulate(now, [h for k in steps for h in (part(left, k), part(right, k + third))])

        for d in range(1, nx):
            peer_copy(own_in, it, d, own_send, own_recv).wait()
        space_in[it, me] = sum_of(own_in, it, nx)
        start_space(lambda s: space_in.at[it, me], space_in, it, space_send, space_recv)

        for copy in turned:
            copy.wait_recv()
        accumulate(now, [h for k in steps for h in (part(right, k), part(left, k + third))])
        for some in (range(third - 1), range(third - 1, third)):
            for k in some:
                onward[2 * k].wait_recv()
                onward[2 * k + 1].wait_recv()
            accumulate(now, [h for k in some for h in (part(across, k), part(across, k + third))])

        for g in range(columns // 128):
            block = zacc[:, pl.ds(g * 128, 128)].reshape(4, 8, 128)
            for t in range(4):
                tiles_out[(g * 4 + t) // per, (g * 4 + t) % per] = block[t]
        start_space(lambda s: tiles_out.at[s], tiles_in, it, tile_send, tile_recv)
        tiles_in[it, me] = tiles_out[me]

        if first:
            turn(high, high_t)
        all_but_one(space_in, it, space_recv.at[it])
        factor_y[...] = inverse_factor(unpack(sum_of(space_in, it, ns)))
        all_but_one(space_in, it, space_send)
        for copy in [*far_copies.values(), *plain_copies.values(), *merged_copies, *spread]:
            copy.wait_send()

        all_but_one(tiles_in, it, tile_recv.at[it])
        sums[it, me] = sum_of(tiles_in, it, ns)
        start_space(lambda s: sums.at[it, me], sums, it, sum_send, sum_recv)
        all_but_one(tiles_in, it, tile_send)
        if first:
            turn(low, low_t)
        all_but_one(sums, it, sum_recv.at[it])
        gathered, blocks = sums[it].reshape(R, 8, 128), []
        for g in range(columns // 128):
            block = gathered[g * 4 : g * 4 + 4].reshape(R, 128)
            blocks.append(block)
        whole = exact(factor_y[...], jnp.concatenate(blocks, axis=1))
        zst[...] = split(whole)
        zfull[...] = whole
        all_but_one(sums, it, sum_send)

    iteration(0, True)

    def later(it, carry):
        iteration(it, False)
        return carry

    lax.fori_loop(1, ITERS + 1, later, 0)

    small[1].wait()
    slices = columns // MODES
    zfull[...] = zfull[...] * (1.0 / math.sqrt(total_rows))
    sketched, rest = [], jnp.zeros((R, MODES), F32)
    for i in range(slices):
        block = zfull[:, pl.ds(i * MODES, MODES)]
        one = exact(following[...], block, NT)
        rest = rest + exact(one, block)
        sketched.append(one)
    sketched = jnp.concatenate(sketched, axis=1)
    last_out[:, pl.ds(0, MODES)] = rest
    last_out[:, pl.ds(MODES, 128)] = jnp.concatenate(
        [exact(sketched, sketched, NT), jnp.zeros((R, 128 - R), F32)], axis=1
    )
    last_in[mx] = last_out[...]

    def last_copy(d):
        return pltpu.make_async_remote_copy(
            src_ref=last_out, dst_ref=last_in.at[mx], send_sem=last_send.at[d - 1], recv_sem=last_recv.at[d - 1],
            device_id=(me, lax.rem(mx + d, nx)), device_id_type=MESH,
        )

    for d in range(1, nx):
        last_copy(d).start()

    def write(h):
        return pltpu.make_async_copy(
            ypart.at[h], basis_out.at[:, pl.ds(h * prows, prows)], out_sem.at[h]
        )

    for q in range(nx):
        some = range(q * PIECES, (q + 1) * PIECES)
        value = jnp.concatenate([yfull[ITERS % 2, h] for h in some], axis=1)
        value = exact(factor_y[...], value) * math.sqrt(total_rows)
        for h in some:
            ypart[h] = value[:, h % PIECES * prows : (h % PIECES + 1) * prows]
            write(h).start()

    for d in range(1, nx):
        last_copy(d).wait()
    total = last_in[0]
    for x in range(1, nx):
        total = total + last_in[x]
    factor = inverse_factor(total[:, MODES : MODES + R])
    second_out[...] = exact(factor, sketched) * math.sqrt(unfold_rows)
    rest_out[...] = exact(factor, total[:, :MODES]) / math.sqrt(unfold_rows)
    for h in range(pieces):
        write(h).wait()


def move(basis, second, rest, basis_out, second_out, rest_out, held, held_second, held_rest, sem, out_sem):
    width = basis.shape[1] // MOVES
    spans = [pl.ds(n * width, width) for n in range(MOVES)]
    ways = [(basis.at[:, at], held.at[:, at], basis_out.at[:, at]) for at in spans]
    ways += [(second, held_second, second_out), (rest, held_rest, rest_out)]
    ins = [pltpu.make_async_copy(a, b, sem.at[n]) for n, (a, b, c) in enumerate(ways)]
    outs = [pltpu.make_async_copy(b, c, out_sem.at[n]) for n, (a, b, c) in enumerate(ways)]
    for copy in ins:
        copy.start()
    for one, other in zip(ins, outs):
        one.wait()
        other.start()
    for copy in outs:
        copy.wait()


def solution(mesh):
    ns, nx = mesh.shape["space"], mesh.shape["param"]

    def shards(snapshots, sketch, following):
        rows, columns = snapshots.shape
        pieces = PIECES * nx
        prows = rows // pieces
        per = R // ns
        slices = columns // MODES
        steps = ITERS + 1
        dma = pltpu.SemaphoreType.DMA
        made = pl.pallas_call(
            functools.partial(kernel, ns, nx, rows * ns, slices * R * nx),
            out_shape=(
                jax.ShapeDtypeStruct((R, rows), F32),
                jax.ShapeDtypeStruct((R, slices * R), F32),
                jax.ShapeDtypeStruct((R, MODES), F32),
            ),
            in_specs=[pl.BlockSpec(memory_space=pl.ANY)] * 3,
            out_specs=(
                pl.BlockSpec(memory_space=pl.ANY),
                pl.BlockSpec(memory_space=pltpu.VMEM),
                pl.BlockSpec(memory_space=pltpu.VMEM),
            ),
            scratch_shapes=[
                pltpu.VMEM((R, columns), F32),
                pltpu.VMEM((R, MODES), F32),
                pltpu.VMEM((pieces, prows, columns), BF16),
                pltpu.VMEM((pieces, prows, columns), BF16),
                pltpu.VMEM((2 * nx, columns, rows // (2 * nx)), BF16),
                pltpu.VMEM((2 * nx, columns, rows // (2 * nx)), BF16),
                pltpu.VMEM((4, prows, columns), F32),
                pltpu.VMEM((2 * R, columns), BF16),
                pltpu.VMEM((pieces, R, prows), F32),
                pltpu.VMEM((2, 2, PIECES // 2, R, prows), F32),
                pltpu.VMEM((2, 2, PIECES, R, prows), F32),
                pltpu.VMEM((2, pieces, R, prows), F32),
                pltpu.VMEM((R, columns), F32),
                pltpu.VMEM((R, columns), F32),
                pltpu.VMEM((ns, per, 8, 128), F32),
                pltpu.VMEM((steps, ns, per, 8, 128), F32),
                pltpu.VMEM((steps, ns, per, 8, 128), F32),
                pltpu.VMEM((steps, nx, 8, 128), F32),
                pltpu.VMEM((steps, nx, 8, 128), F32),
                pltpu.VMEM((steps, ns, 8, 128), F32),
                pltpu.VMEM((R, MODES + 128), F32),
                pltpu.VMEM((nx, R, MODES + 128), F32),
                pltpu.VMEM((R, R), F32),
                dma((2,)),
                dma((4,)),
                dma((36,)),
                dma((steps, 36)),
                dma,
                dma((steps,)),
                dma,
                dma((steps,)),
                dma((nx - 1,)),
                dma((steps, nx - 1)),
                dma((nx - 1,)),
                dma((steps, nx - 1)),
                dma,
                dma((steps,)),
                dma((nx - 1,)),
                dma((nx - 1,)),
                dma((pieces,)),
            ],
            compiler_params=pltpu.CompilerParams(
                collective_id=0, has_side_effects=True, vmem_limit_bytes=60 * 1024 * 1024
            ),
        )(snapshots, sketch.T, following.T)
        anywhere = pl.BlockSpec(memory_space=pl.ANY)
        return pl.pallas_call(
            move,
            out_shape=tuple(jax.ShapeDtypeStruct(one.shape, F32) for one in made),
            in_specs=[anywhere] * 3,
            out_specs=(anywhere,) * 3,
            scratch_shapes=[pltpu.VMEM(one.shape, F32) for one in made] + [dma((MOVES + 2,)), dma((MOVES + 2,))],
        )(*made)

    return jax.shard_map(
        shards,
        mesh=mesh,
        in_specs=(P("space", "param"), P("param", None), P()),
        out_specs=(P(None, "space"), P(None, "param"), P()),
        check_vma=False,
    )
```

```python
import functools
import math

import jax
import jax.numpy as jnp
from jax import lax
from jax.experimental import pallas as pl
from jax.experimental.pallas import tpu as pltpu
from jax.sharding import PartitionSpec as P

MESH = pl.DeviceIdType.MESH
R = 32
MOVES = 4
MODES = 256
ITERS = 3
BLOCK = 8
PIECES = 6
F32, BF16 = jnp.float32, jnp.bfloat16
NN = (((1,), (0,)), ((), ()))
NT = (((1,), (1,)), ((), ()))


def exact(a, b, dims=NN):
    return lax.dot_general(a, b, dims, precision=lax.Precision.HIGHEST, preferred_element_type=F32)


def split(value):
    high = value.astype(BF16)
    low = (value - high.astype(F32)).astype(BF16)
    return jnp.concatenate([high, low], axis=0)


def fold(pair):
    return pair[:R] + pair[R:]


def gram_of(stacked):
    both = lax.dot_general(stacked, stacked, NT, preferred_element_type=F32)
    half = fold(both)
    return half[:, :R] + half[:, R:]


def inverse_factor(gram):
    wide = (R, 2 * R)
    rows = lax.broadcasted_iota(jnp.int32, (R, R), 0)
    columns = lax.broadcasted_iota(jnp.int32, (R, R), 1)
    eye = jnp.where(rows == columns, 1.0, 0.0).astype(F32)
    work = jnp.concatenate([gram, eye], axis=1)
    below = lax.broadcasted_iota(jnp.int32, wide, 0)
    for j in range(0, R, BLOCK):
        row = [work[j + i : j + i + 1, :] for i in range(BLOCK)]
        spread = [[jnp.broadcast_to(row[i][:, j + k : j + k + 1], (1, 2 * R)) for k in range(BLOCK)] for i in range(BLOCK)]
        column = [jnp.broadcast_to(work[:, j + i : j + i + 1], wide) for i in range(BLOCK)]
        for i in range(BLOCK):
            if j + i == R - 1:
                break
            inverse = 1.0 / spread[i][i]
            scaled = row[i] * inverse
            work = work - jnp.where(below > j + i, column[i], 0.0) * scaled
            for k in range(i + 1, BLOCK):
                ratio = spread[i][k] * inverse
                row[k] = row[k] - spread[i][k] * scaled
                column[k] = column[k] - column[i] * ratio
                for m in range(k, BLOCK):
                    spread[k][m] = spread[k][m] - spread[i][m] * ratio
    diagonal = jnp.sum(jnp.where(rows == columns, work[:, :R], 0.0), axis=1, keepdims=True)
    return work[:, R:] / jnp.sqrt(diagonal)


def pack(square):
    return jnp.concatenate([square[8 * i : 8 * i + 8] for i in range(4)], axis=1)


def unpack(tile):
    return jnp.concatenate([tile[:, R * i : R * i + R] for i in range(4)], axis=0)


def kernel(
    ns, nx, total_rows, unfold_rows,
    snap, sketch_in, following_in, basis_out, second_out, rest_out,
    sketch, following, high, low, high_t, low_t, stage, zst, ypart, first_in, second_in, yfull, zacc, zfull,
    tiles_out, tiles_in, sums, gram_in, own_in, space_in, last_out, last_in,
    factor_y,
    small_sem, load_sem, send_sem, recv_sem, tile_send, tile_recv, sum_send, sum_recv,
    gram_send, gram_recv, own_send, own_recv, space_send, space_recv, last_send, last_recv, out_sem,
):
    me, mx = lax.axis_index("space"), lax.axis_index("param")
    right, left, across = lax.rem(mx + 1, nx), lax.rem(mx + nx - 1, nx), lax.rem(mx + 2, nx)
    pieces, prows, columns = high.shape
    per = tiles_out.shape[1]
    third = PIECES // 2
    loads = stage.shape[0]

    def part(quarter, piece):
        return quarter * PIECES + piece

    steps = range(third)
    far = [part(across, k + side * third) for k in steps for side in (0, 1)]
    plain = [h for k in steps for h in (part(right, k + third), part(left, k))]
    merged = [h for k in steps for h in (part(right, k), part(left, k + third))]
    own = [part(mx, k + side * third) for k in steps for side in (0, 1)]
    order = far + plain + merged + own
    quarters = [across] * 6 + [right, left] * 6 + [mx] * 6
    sides = [0, 1] * third + [1, 0] * third + [0, 1] * third * 2
    places = [(quarters[n] * 2 + sides[n], n % 6 // 2) for n in range(4 * PIECES)]

    def load(n):
        return pltpu.make_async_copy(
            snap.at[pl.ds(pl.multiple_of(order[n] * prows, prows), prows), :],
            stage.at[n % loads], load_sem.at[n % loads],
        )

    small = [
        pltpu.make_async_copy(sketch_in, sketch, small_sem.at[0]),
        pltpu.make_async_copy(following_in, following, small_sem.at[1]),
    ]
    small[0].start()
    for n in range(loads):
        load(n).start()
    small[1].start()

    barrier = pltpu.get_barrier_semaphore()

    def greet(d, carry):
        pl.semaphore_signal(barrier, inc=1, device_id=(lax.rem(me + d, ns), mx), device_id_type=MESH)
        return carry

    lax.fori_loop(1, ns, greet, 0)
    for d in range(1, nx):
        pl.semaphore_signal(barrier, inc=1, device_id=(me, lax.rem(mx + d, nx)), device_id_type=MESH)

    small[0].wait()
    zst[...] = split(sketch[...])

    def product(n, first):
        h = order[n]
        if first:
            load(n).wait()
            value = stage[n % loads]
            top = value.astype(BF16)
            rest = (value - top.astype(F32)).astype(BF16)
            high[h] = top
            low[h] = rest
            pair = lax.dot_general(zst[...], top, NT, preferred_element_type=F32)
            pair += lax.dot_general(zst[...], rest, NT, preferred_element_type=F32)
            if n + loads < pieces:
                load(n + loads).start()
        else:
            side, k = places[n]
            at = pl.ds(k * prows, prows)
            pair = lax.dot_general(zst[...], high_t[side, :, at], NN, preferred_element_type=F32)
            pair += lax.dot_general(zst[...], low_t[side, :, at], NN, preferred_element_type=F32)
        return fold(pair)

    def turn(source, target):
        def one(i, carry):
            for b in range(columns // 256):
                at = pl.ds(b * 256, 256)
                rows = [source[i * third + k, :, at] for k in steps]
                target[i, at, :] = jnp.concatenate(rows, axis=0).T
            return carry

        lax.fori_loop(0, pieces // third, one, 0)

    def in_turn(numbers, first, ready):
        ahead = None
        for n in numbers:
            value = product(n, first)
            if ahead is not None:
                ready(*ahead)
            ahead = (n, value)
        ready(*ahead)

    def along_x(source, target, n, it, x):
        return pltpu.make_async_remote_copy(
            src_ref=source, dst_ref=target, send_sem=send_sem.at[n], recv_sem=recv_sem.at[it, n],
            device_id=(me, x), device_id_type=MESH,
        )

    def accumulate(it, some):
        stacked = [split(yfull[it, h]) for h in some]
        for b in range(columns // 256):
            at = pl.ds(b * 256, 256)
            pair = None
            for a, h in zip(stacked, some):
                one = lax.dot_general(a, high[h, :, at], NN, preferred_element_type=F32)
                one += lax.dot_general(a, low[h, :, at], NN, preferred_element_type=F32)
                pair = one if pair is None else pair + one
            zacc[:, at] += fold(pair)
        return stacked

    def peer_copy(ref, it, d, send, recv):
        return pltpu.make_async_remote_copy(
            src_ref=ref.at[it, mx], dst_ref=ref.at[it, mx], send_sem=send.at[d - 1], recv_sem=recv.at[it, d - 1],
            device_id=(me, lax.rem(mx + d, nx)), device_id_type=MESH,
        )

    nc = 2
    nz = min(4, ns // nc)
    ny = ns // (nc * nz)
    myy, myz, myc = me // (nz * nc), me // nc % nz, me % nc
    hops = sorted(
        (-min(dy, ny - dy) - min(dz, nz - dz), dy, dz, dc)
        for dy in range(ny) for dz in range(nz) for dc in range(nc) if dy or dz or dc
    )
    others = [
        ((lax.rem(myy + dy, ny) * nz + lax.rem(myz + dz, nz)) * nc + lax.rem(myc + dc, nc)) for _, dy, dz, dc in hops
    ]

    def start_space(source, ref, it, send, recv):
        for s in others:
            pltpu.make_async_remote_copy(
                src_ref=source(s), dst_ref=ref.at[it, me], send_sem=send, recv_sem=recv.at[it],
                device_id=(s, mx), device_id_type=MESH,
            ).start()

    def all_but_one(ref, it, sem):
        some = ref.at[it, pl.ds(0, ns - 1)]
        pltpu.make_async_copy(some, some, sem).wait()

    def sum_of(ref, it, count):
        total = ref[it, 0]
        for x in range(1, count):
            total = total + ref[it, x]
        return total

    def iteration(it, first):
        now = it % 2
        far_copies, plain_copies, merged_copies = {}, {}, []

        def send_far(n, value):
            k, side = divmod(n, 2)
            if not first:
                ypart[order[n]] = value
            copy = along_x(ypart.at[order[n]], first_in.at[now, side, k], n, it, left if side else right)
            copy.start()
            far_copies[n] = copy

        def send_plain(n, value):
            k, side = divmod(n - len(far), 2)
            ypart[order[n]] = value
            slot = second_in.at[now, side, k if side else k + third]
            copy = along_x(ypart.at[order[n]], slot, n, it, left if side else right)
            copy.start()
            plain_copies[n - len(far)] = copy

        def keep(n, value):
            ypart[order[n]] = value

        begun, base = len(far) + len(plain), pieces - len(own)
        if first:
            in_turn(range(len(far)), first, keep)
            pl.semaphore_wait(barrier, ns - 1 + nx - 1)
            for n in range(len(far)):
                send_far(n, None)
        else:
            in_turn(range(2), first, send_far)
            gram_in[it, mx] = pack(gram_of(zst[...]))
            for d in range(1, nx):
                peer_copy(gram_in, it, d, gram_send, gram_recv).start()
            in_turn(range(2, len(far)), first, send_far)
        in_turn(range(len(far), begun), first, send_plain)
        in_turn(range(begun, base), first, keep)
        for m, h in enumerate(merged):
            k, side = divmod(m, 2)
            far_copies[m].wait_recv()
            ypart[h] += first_in[now, side, k]
            slot = second_in.at[now, side, k + third if side else k]
            copy = along_x(ypart.at[h], slot, begun + m, it, left if side else right)
            copy.start()
            merged_copies.append(copy)

        if first:
            factor = None
        else:
            for d in range(1, nx):
                peer_copy(gram_in, it, d, gram_send, gram_recv).wait()
            factor = inverse_factor(unpack(sum_of(gram_in, it, nx)))
        in_turn(range(base, pieces), first, keep)

        spread = []

        def send_own(h, n, x):
            copy = along_x(yfull.at[now, h], yfull.at[now, h], n, it, x)
            copy.start()
            spread.append(copy)
            return copy

        straight, turned, values = [], [], []

        def cross(k):
            for m in (2 * k, 2 * k + 1):
                turned.append(send_own(own[m], 24 + m, right if m % 2 else left))

        for k in steps:
            value = []
            for m in (2 * k, 2 * k + 1):
                merged_copies[m].wait_recv()
                plain_copies[m].wait_recv()
            for m in (2 * k, 2 * k + 1):
                piece = k + m % 2 * third
                value.append(ypart[own[m]] + second_in[now, 0, piece] + second_in[now, 1, piece])
            value = jnp.concatenate(value, axis=1)
            if factor is not None:
                value = exact(factor, value)
            values.append(value)
            for m in (2 * k, 2 * k + 1):
                yfull[now, own[m]] = value[:, m % 2 * prows : (m % 2 + 1) * prows]
                straight.append(send_own(own[m], 18 + m, left if m % 2 else right))
        own_in[it, mx] = pack(gram_of(split(jnp.concatenate(values, axis=1))))
        for d in range(1, nx):
            peer_copy(own_in, it, d, own_send, own_recv).start()
        for k in steps:
            cross(k)
        zacc[...] = jnp.zeros_like(zacc)
        accumulate(now, own)
        onward = []
        for k in steps:
            straight[2 * k].wait_recv()
            onward.append(send_own(part(left, k), 30 + 2 * k, right))
            straight[2 * k + 1].wait_recv()
            onward.append(send_own(part(right, k + third), 31 + 2 * k, left))
        accumulate(now, [h for k in steps for h in (part(left, k), part(right, k + third))])

        for d in range(1, nx):
            peer_copy(own_in, it, d, own_send, own_recv).wait()
        space_in[it, me] = sum_of(own_in, it, nx)
        start_space(lambda s: space_in.at[it, me], space_in, it, space_send, space_recv)

        for k in steps:
            turned[2 * k].wait_recv()
            turned[2 * k + 1].wait_recv()
            accumulate(now, [part(right, k), part(left, k + third)])
        for k in steps:
            onward[2 * k].wait_recv()
            onward[2 * k + 1].wait_recv()
            accumulate(now, [part(across, k), part(across, k + third)])

        for g in range(columns // 128):
            block = zacc[:, pl.ds(g * 128, 128)].reshape(4, 8, 128)
            for t in range(4):
                tiles_out[(g * 4 + t) // per, (g * 4 + t) % per] = block[t]
        start_space(lambda s: tiles_out.at[s], tiles_in, it, tile_send, tile_recv)
        tiles_in[it, me] = tiles_out[me]

        if first:
            turn(high, high_t)
        all_but_one(space_in, it, space_recv.at[it])
        factor_y[...] = inverse_factor(unpack(sum_of(space_in, it, ns)))
        all_but_one(space_in, it, space_send)
        for copy in [*far_copies.values(), *plain_copies.values(), *merged_copies, *spread]:
            copy.wait_send()

        all_but_one(tiles_in, it, tile_recv.at[it])
        sums[it, me] = sum_of(tiles_in, it, ns)
        start_space(lambda s: sums.at[it, me], sums, it, sum_send, sum_recv)
        all_but_one(tiles_in, it, tile_send)
        if first:
            turn(low, low_t)
        all_but_one(sums, it, sum_recv.at[it])
        gathered, blocks = sums[it].reshape(R, 8, 128), []
        for g in range(columns // 128):
            block = gathered[g * 4 : g * 4 + 4].reshape(R, 128)
            blocks.append(block)
        whole = exact(factor_y[...], jnp.concatenate(blocks, axis=1))
        zst[...] = split(whole)
        zfull[...] = whole
        all_but_one(sums, it, sum_send)

    iteration(0, True)

    def later(it, carry):
        iteration(it, False)
        return carry

    lax.fori_loop(1, ITERS + 1, later, 0)

    small[1].wait()
    slices = columns // MODES
    zfull[...] = zfull[...] * (1.0 / math.sqrt(total_rows))
    sketched, rest = [], jnp.zeros((R, MODES), F32)
    for i in range(slices):
        block = zfull[:, pl.ds(i * MODES, MODES)]
        one = exact(following[...], block, NT)
        rest = rest + exact(one, block)
        sketched.append(one)
    sketched = jnp.concatenate(sketched, axis=1)
    last_out[:, pl.ds(0, MODES)] = rest
    last_out[:, pl.ds(MODES, 128)] = jnp.concatenate(
        [exact(sketched, sketched, NT), jnp.zeros((R, 128 - R), F32)], axis=1
    )
    last_in[mx] = last_out[...]

    def last_copy(d):
        return pltpu.make_async_remote_copy(
            src_ref=last_out, dst_ref=last_in.at[mx], send_sem=last_send.at[d - 1], recv_sem=last_recv.at[d - 1],
            device_id=(me, lax.rem(mx + d, nx)), device_id_type=MESH,
        )

    for d in range(1, nx):
        last_copy(d).start()

    def write(h):
        return pltpu.make_async_copy(
            ypart.at[h], basis_out.at[:, pl.ds(h * prows, prows)], out_sem.at[h]
        )

    for q in range(nx):
        some = range(q * PIECES, (q + 1) * PIECES)
        value = jnp.concatenate([yfull[ITERS % 2, h] for h in some], axis=1)
        value = exact(factor_y[...], value) * math.sqrt(total_rows)
        for h in some:
            ypart[h] = value[:, h % PIECES * prows : (h % PIECES + 1) * prows]
            write(h).start()

    for d in range(1, nx):
        last_copy(d).wait()
    total = last_in[0]
    for x in range(1, nx):
        total = total + last_in[x]
    factor = inverse_factor(total[:, MODES : MODES + R])
    second_out[...] = exact(factor, sketched) * math.sqrt(unfold_rows)
    rest_out[...] = exact(factor, total[:, :MODES]) / math.sqrt(unfold_rows)
    for h in range(pieces):
        write(h).wait()


def move(basis, second, rest, basis_out, second_out, rest_out, held, held_second, held_rest, sem, out_sem):
    width = basis.shape[1] // MOVES
    spans = [pl.ds(n * width, width) for n in range(MOVES)]
    ways = [(basis.at[:, at], held.at[:, at], basis_out.at[:, at]) for at in spans]
    ways += [(second, held_second, second_out), (rest, held_rest, rest_out)]
    ins = [pltpu.make_async_copy(a, b, sem.at[n]) for n, (a, b, c) in enumerate(ways)]
    outs = [pltpu.make_async_copy(b, c, out_sem.at[n]) for n, (a, b, c) in enumerate(ways)]
    for copy in ins:
        copy.start()
    for one, other in zip(ins, outs):
        one.wait()
        other.start()
    for copy in outs:
        copy.wait()


def solution(mesh):
    ns, nx = mesh.shape["space"], mesh.shape["param"]

    def shards(snapshots, sketch, following):
        rows, columns = snapshots.shape
        pieces = PIECES * nx
        prows = rows // pieces
        per = R // ns
        slices = columns // MODES
        steps = ITERS + 1
        dma = pltpu.SemaphoreType.DMA
        made = pl.pallas_call(
            functools.partial(kernel, ns, nx, rows * ns, slices * R * nx),
            out_shape=(
                jax.ShapeDtypeStruct((R, rows), F32),
                jax.ShapeDtypeStruct((R, slices * R), F32),
                jax.ShapeDtypeStruct((R, MODES), F32),
            ),
            in_specs=[pl.BlockSpec(memory_space=pl.ANY)] * 3,
            out_specs=(
                pl.BlockSpec(memory_space=pl.ANY),
                pl.BlockSpec(memory_space=pltpu.VMEM),
                pl.BlockSpec(memory_space=pltpu.VMEM),
            ),
            scratch_shapes=[
                pltpu.VMEM((R, columns), F32),
                pltpu.VMEM((R, MODES), F32),
                pltpu.VMEM((pieces, prows, columns), BF16),
                pltpu.VMEM((pieces, prows, columns), BF16),
                pltpu.VMEM((2 * nx, columns, rows // (2 * nx)), BF16),
                pltpu.VMEM((2 * nx, columns, rows // (2 * nx)), BF16),
                pltpu.VMEM((4, prows, columns), F32),
                pltpu.VMEM((2 * R, columns), BF16),
                pltpu.VMEM((pieces, R, prows), F32),
                pltpu.VMEM((2, 2, PIECES // 2, R, prows), F32),
                pltpu.VMEM((2, 2, PIECES, R, prows), F32),
                pltpu.VMEM((2, pieces, R, prows), F32),
                pltpu.VMEM((R, columns), F32),
                pltpu.VMEM((R, columns), F32),
                pltpu.VMEM((ns, per, 8, 128), F32),
                pltpu.VMEM((steps, ns, per, 8, 128), F32),
                pltpu.VMEM((steps, ns, per, 8, 128), F32),
                pltpu.VMEM((steps, nx, 8, 128), F32),
                pltpu.VMEM((steps, nx, 8, 128), F32),
                pltpu.VMEM((steps, ns, 8, 128), F32),
                pltpu.VMEM((R, MODES + 128), F32),
                pltpu.VMEM((nx, R, MODES + 128), F32),
                pltpu.VMEM((R, R), F32),
                dma((2,)),
                dma((4,)),
                dma((36,)),
                dma((steps, 36)),
                dma,
                dma((steps,)),
                dma,
                dma((steps,)),
                dma((nx - 1,)),
                dma((steps, nx - 1)),
                dma((nx - 1,)),
                dma((steps, nx - 1)),
                dma,
                dma((steps,)),
                dma((nx - 1,)),
                dma((nx - 1,)),
                dma((pieces,)),
            ],
            compiler_params=pltpu.CompilerParams(
                collective_id=0, has_side_effects=True, vmem_limit_bytes=60 * 1024 * 1024
            ),
        )(snapshots, sketch.T, following.T)
        anywhere = pl.BlockSpec(memory_space=pl.ANY)
        return pl.pallas_call(
            move,
            out_shape=tuple(jax.ShapeDtypeStruct(one.shape, F32) for one in made),
            in_specs=[anywhere] * 3,
            out_specs=(anywhere,) * 3,
            scratch_shapes=[pltpu.VMEM(one.shape, F32) for one in made] + [dma((MOVES + 2,)), dma((MOVES + 2,))],
        )(*made)

    return jax.shard_map(
        shards,
        mesh=mesh,
        in_specs=(P("space", "param"), P("param", None), P()),
        out_specs=(P(None, "space"), P(None, "param"), P()),
        check_vma=False,
    )
```

```python
import functools
import math

import jax
import jax.numpy as jnp
from jax import lax
from jax.experimental import pallas as pl
from jax.experimental.pallas import tpu as pltpu
from jax.sharding import PartitionSpec as P

MESH = pl.DeviceIdType.MESH
R = 32
MOVES = 4
MODES = 256
ITERS = 3
BLOCK = 8
PIECES = 6
F32, BF16 = jnp.float32, jnp.bfloat16
NN = (((1,), (0,)), ((), ()))
NT = (((1,), (1,)), ((), ()))


def exact(a, b, dims=NN):
    return lax.dot_general(a, b, dims, precision=lax.Precision.HIGHEST, preferred_element_type=F32)


def split(value):
    high = value.astype(BF16)
    low = (value - high.astype(F32)).astype(BF16)
    return jnp.concatenate([high, low], axis=0)


def fold(pair):
    return pair[:R] + pair[R:]


def gram_of(stacked):
    both = lax.dot_general(stacked, stacked, NT, preferred_element_type=F32)
    half = fold(both)
    return half[:, :R] + half[:, R:]


def inverse_factor(gram):
    wide = (R, 2 * R)
    rows = lax.broadcasted_iota(jnp.int32, (R, R), 0)
    columns = lax.broadcasted_iota(jnp.int32, (R, R), 1)
    eye = jnp.where(rows == columns, 1.0, 0.0).astype(F32)
    work = jnp.concatenate([gram, eye], axis=1)
    below = lax.broadcasted_iota(jnp.int32, wide, 0)
    for j in range(0, R, BLOCK):
        row = [work[j + i : j + i + 1, :] for i in range(BLOCK)]
        spread = [[jnp.broadcast_to(row[i][:, j + k : j + k + 1], (1, 2 * R)) for k in range(BLOCK)] for i in range(BLOCK)]
        column = [jnp.broadcast_to(work[:, j + i : j + i + 1], wide) for i in range(BLOCK)]
        for i in range(BLOCK):
            if j + i == R - 1:
                break
            inverse = 1.0 / spread[i][i]
            scaled = row[i] * inverse
            work = work - jnp.where(below > j + i, column[i], 0.0) * scaled
            for k in range(i + 1, BLOCK):
                ratio = spread[i][k] * inverse
                row[k] = row[k] - spread[i][k] * scaled
                column[k] = column[k] - column[i] * ratio
                for m in range(k, BLOCK):
                    spread[k][m] = spread[k][m] - spread[i][m] * ratio
    diagonal = jnp.sum(jnp.where(rows == columns, work[:, :R], 0.0), axis=1, keepdims=True)
    return work[:, R:] / jnp.sqrt(diagonal)


def pack(square):
    return jnp.concatenate([square[8 * i : 8 * i + 8] for i in range(4)], axis=1)


def unpack(tile):
    return jnp.concatenate([tile[:, R * i : R * i + R] for i in range(4)], axis=0)


def kernel(
    ns, nx, total_rows, unfold_rows,
    snap, sketch_in, following_in, basis_out, second_out, rest_out,
    sketch, following, high, low, high_t, low_t, stage, zst, ypart, first_in, second_in, yfull, zacc, zfull,
    tiles_out, tiles_in, sums, gram_in, own_in, space_in, last_out, last_in,
    factor_y,
    small_sem, load_sem, send_sem, recv_sem, tile_send, tile_recv, sum_send, sum_recv,
    gram_send, gram_recv, own_send, own_recv, space_send, space_recv, last_send, last_recv, out_sem,
):
    me, mx = lax.axis_index("space"), lax.axis_index("param")
    right, left, across = lax.rem(mx + 1, nx), lax.rem(mx + nx - 1, nx), lax.rem(mx + 2, nx)
    pieces, prows, columns = high.shape
    per = tiles_out.shape[1]
    third = PIECES // 2
    loads = stage.shape[0]

    def part(quarter, piece):
        return quarter * PIECES + piece

    steps = range(third)
    far = [part(across, k + side * third) for k in steps for side in (0, 1)]
    plain = [h for k in steps for h in (part(right, k + third), part(left, k))]
    merged = [h for k in steps for h in (part(right, k), part(left, k + third))]
    own = [part(mx, k + side * third) for k in steps for side in (0, 1)]
    order = far + plain + merged + own
    quarters = [across] * 6 + [right, left] * 6 + [mx] * 6
    sides = [0, 1] * third + [1, 0] * third + [0, 1] * third * 2
    places = [(quarters[n] * 2 + sides[n], n % 6 // 2) for n in range(4 * PIECES)]

    def load(n):
        return pltpu.make_async_copy(
            snap.at[pl.ds(pl.multiple_of(order[n] * prows, prows), prows), :],
            stage.at[n % loads], load_sem.at[n % loads],
        )

    small = [
        pltpu.make_async_copy(sketch_in, sketch, small_sem.at[0]),
        pltpu.make_async_copy(following_in, following, small_sem.at[1]),
    ]
    small[0].start()
    for n in range(loads):
        load(n).start()
    small[1].start()

    barrier = pltpu.get_barrier_semaphore()

    def greet(d, carry):
        pl.semaphore_signal(barrier, inc=1, device_id=(lax.rem(me + d, ns), mx), device_id_type=MESH)
        return carry

    lax.fori_loop(1, ns, greet, 0)
    for d in range(1, nx):
        pl.semaphore_signal(barrier, inc=1, device_id=(me, lax.rem(mx + d, nx)), device_id_type=MESH)

    small[0].wait()
    zst[...] = split(sketch[...])

    def product(n, first):
        h = order[n]
        if first:
            load(n).wait()
            value = stage[n % loads]
            top = value.astype(BF16)
            rest = (value - top.astype(F32)).astype(BF16)
            high[h] = top
            low[h] = rest
            pair = lax.dot_general(zst[...], top, NT, preferred_element_type=F32)
            pair += lax.dot_general(zst[...], rest, NT, preferred_element_type=F32)
            if n + loads < pieces:
                load(n + loads).start()
        else:
            side, k = places[n]
            at = pl.ds(k * prows, prows)
            pair = lax.dot_general(zst[...], high_t[side, :, at], NN, preferred_element_type=F32)
            pair += lax.dot_general(zst[...], low_t[side, :, at], NN, preferred_element_type=F32)
        return fold(pair)

    def turn(source, target):
        def one(i, carry):
            for b in range(columns // 256):
                at = pl.ds(b * 256, 256)
                rows = [source[i * third + k, :, at] for k in steps]
                target[i, at, :] = jnp.concatenate(rows, axis=0).T
            return carry

        lax.fori_loop(0, pieces // third, one, 0)

    def in_turn(numbers, first, ready):
        ahead = None
        for n in numbers:
            value = product(n, first)
            if ahead is not None:
                ready(*ahead)
            ahead = (n, value)
        ready(*ahead)

    def along_x(source, target, n, it, x):
        return pltpu.make_async_remote_copy(
            src_ref=source, dst_ref=target, send_sem=send_sem.at[n], recv_sem=recv_sem.at[it, n],
            device_id=(me, x), device_id_type=MESH,
        )

    def accumulate(it, some):
        stacked = [split(yfull[it, h]) for h in some]
        for b in range(columns // 256):
            at = pl.ds(b * 256, 256)
            pair = None
            for a, h in zip(stacked, some):
                one = lax.dot_general(a, high[h, :, at], NN, preferred_element_type=F32)
                one += lax.dot_general(a, low[h, :, at], NN, preferred_element_type=F32)
                pair = one if pair is None else pair + one
            zacc[:, at] += fold(pair)
        return stacked

    def peer_copy(ref, it, d, send, recv):
        return pltpu.make_async_remote_copy(
            src_ref=ref.at[it, mx], dst_ref=ref.at[it, mx], send_sem=send.at[d - 1], recv_sem=recv.at[it, d - 1],
            device_id=(me, lax.rem(mx + d, nx)), device_id_type=MESH,
        )

    nc = 2
    nz = min(4, ns // nc)
    ny = ns // (nc * nz)
    myy, myz, myc = me // (nz * nc), me // nc % nz, me % nc
    hops = sorted(
        (-min(dy, ny - dy) - min(dz, nz - dz), dy, dz, dc)
        for dy in range(ny) for dz in range(nz) for dc in range(nc) if dy or dz or dc
    )
    others = [
        ((lax.rem(myy + dy, ny) * nz + lax.rem(myz + dz, nz)) * nc + lax.rem(myc + dc, nc)) for _, dy, dz, dc in hops
    ]

    def start_space(source, ref, it, send, recv):
        for s in others:
            pltpu.make_async_remote_copy(
                src_ref=source(s), dst_ref=ref.at[it, me], send_sem=send, recv_sem=recv.at[it],
                device_id=(s, mx), device_id_type=MESH,
            ).start()

    def all_but_one(ref, it, sem):
        some = ref.at[it, pl.ds(0, ns - 1)]
        pltpu.make_async_copy(some, some, sem).wait()

    def sum_of(ref, it, count):
        total = ref[it, 0]
        for x in range(1, count):
            total = total + ref[it, x]
        return total

    def iteration(it, first):
        now = it % 2
        far_copies, plain_copies, merged_copies = {}, {}, []

        def send_far(n, value):
            k, side = divmod(n, 2)
            if not first:
                ypart[order[n]] = value
            copy = along_x(ypart.at[order[n]], first_in.at[now, side, k], n, it, left if side else right)
            copy.start()
            far_copies[n] = copy

        def send_plain(n, value):
            k, side = divmod(n - len(far), 2)
            ypart[order[n]] = value
            slot = second_in.at[now, side, k if side else k + third]
            copy = along_x(ypart.at[order[n]], slot, n, it, left if side else right)
            copy.start()
            plain_copies[n - len(far)] = copy

        def keep(n, value):
            ypart[order[n]] = value

        begun, base = len(far) + len(plain), pieces - len(own)
        if first:
            in_turn(range(len(far)), first, keep)
            pl.semaphore_wait(barrier, ns - 1 + nx - 1)
            for n in range(len(far)):
                send_far(n, None)
        else:
            in_turn(range(2), first, send_far)
            gram_in[it, mx] = pack(gram_of(zst[...]))
            for d in range(1, nx):
                peer_copy(gram_in, it, d, gram_send, gram_recv).start()
            in_turn(range(2, len(far)), first, send_far)
        in_turn(range(len(far), begun), first, send_plain)
        in_turn(range(begun, base), first, keep)
        for m, h in enumerate(merged):
            k, side = divmod(m, 2)
            far_copies[m].wait_recv()
            ypart[h] += first_in[now, side, k]
            slot = second_in.at[now, side, k + third if side else k]
            copy = along_x(ypart.at[h], slot, begun + m, it, left if side else right)
            copy.start()
            merged_copies.append(copy)

        if first:
            factor = None
        else:
            for d in range(1, nx):
                peer_copy(gram_in, it, d, gram_send, gram_recv).wait()
            factor = inverse_factor(unpack(sum_of(gram_in, it, nx)))
        in_turn(range(base, pieces), first, keep)

        spread = []

        def send_own(h, n, x):
            copy = along_x(yfull.at[now, h], yfull.at[now, h], n, it, x)
            copy.start()
            spread.append(copy)
            return copy

        straight, turned, values = [], [], []

        def cross(k):
            for m in (2 * k, 2 * k + 1):
                turned.append(send_own(own[m], 24 + m, right if m % 2 else left))

        for k in steps:
            value = []
            for m in (2 * k, 2 * k + 1):
                merged_copies[m].wait_recv()
                plain_copies[m].wait_recv()
            for m in (2 * k, 2 * k + 1):
                piece = k + m % 2 * third
                value.append(ypart[own[m]] + second_in[now, 0, piece] + second_in[now, 1, piece])
            value = jnp.concatenate(value, axis=1)
            if factor is not None:
                value = exact(factor, value)
            values.append(value)
            for m in (2 * k, 2 * k + 1):
                yfull[now, own[m]] = value[:, m % 2 * prows : (m % 2 + 1) * prows]
                straight.append(send_own(own[m], 18 + m, left if m % 2 else right))
        own_in[it, mx] = pack(gram_of(split(jnp.concatenate(values, axis=1))))
        for d in range(1, nx):
            peer_copy(own_in, it, d, own_send, own_recv).start()
        for k in steps:
            cross(k)
        zacc[...] = jnp.zeros_like(zacc)
        accumulate(now, own)
        onward = []
        for k in steps:
            straight[2 * k].wait_recv()
            onward.append(send_own(part(left, k), 30 + 2 * k, right))
            straight[2 * k + 1].wait_recv()
            onward.append(send_own(part(right, k + third), 31 + 2 * k, left))
            accumulate(now, [part(left, k), part(right, k + third)])

        for d in range(1, nx):
            peer_copy(own_in, it, d, own_send, own_recv).wait()
        space_in[it, me] = sum_of(own_in, it, nx)
        start_space(lambda s: space_in.at[it, me], space_in, it, space_send, space_recv)

        for k in steps:
            turned[2 * k].wait_recv()
            turned[2 * k + 1].wait_recv()
            accumulate(now, [part(right, k), part(left, k + third)])
        for k in steps:
            onward[2 * k].wait_recv()
            onward[2 * k + 1].wait_recv()
            accumulate(now, [part(across, k), part(across, k + third)])

        for g in range(columns // 128):
            block = zacc[:, pl.ds(g * 128, 128)].reshape(4, 8, 128)
            for t in range(4):
                tiles_out[(g * 4 + t) // per, (g * 4 + t) % per] = block[t]
        start_space(lambda s: tiles_out.at[s], tiles_in, it, tile_send, tile_recv)
        tiles_in[it, me] = tiles_out[me]

        if first:
            turn(high, high_t)
        all_but_one(space_in, it, space_recv.at[it])
        factor_y[...] = inverse_factor(unpack(sum_of(space_in, it, ns)))
        all_but_one(space_in, it, space_send)
        for copy in [*far_copies.values(), *plain_copies.values(), *merged_copies, *spread]:
            copy.wait_send()

        all_but_one(tiles_in, it, tile_recv.at[it])
        sums[it, me] = sum_of(tiles_in, it, ns)
        start_space(lambda s: sums.at[it, me], sums, it, sum_send, sum_recv)
        all_but_one(tiles_in, it, tile_send)
        if first:
            turn(low, low_t)
        all_but_one(sums, it, sum_recv.at[it])
        gathered, blocks = sums[it].reshape(R, 8, 128), []
        for g in range(columns // 128):
            block = gathered[g * 4 : g * 4 + 4].reshape(R, 128)
            blocks.append(block)
        whole = exact(factor_y[...], jnp.concatenate(blocks, axis=1))
        zst[...] = split(whole)
        zfull[...] = whole
        all_but_one(sums, it, sum_send)

    iteration(0, True)

    def later(it, carry):
        iteration(it, False)
        return carry

    lax.fori_loop(1, ITERS + 1, later, 0)

    small[1].wait()
    slices = columns // MODES
    zfull[...] = zfull[...] * (1.0 / math.sqrt(total_rows))
    sketched, rest = [], jnp.zeros((R, MODES), F32)
    for i in range(slices):
        block = zfull[:, pl.ds(i * MODES, MODES)]
        one = exact(following[...], block, NT)
        rest = rest + exact(one, block)
        sketched.append(one)
    sketched = jnp.concatenate(sketched, axis=1)
    last_out[:, pl.ds(0, MODES)] = rest
    last_out[:, pl.ds(MODES, 128)] = jnp.concatenate(
        [exact(sketched, sketched, NT), jnp.zeros((R, 128 - R), F32)], axis=1
    )
    last_in[mx] = last_out[...]

    def last_copy(d):
        return pltpu.make_async_remote_copy(
            src_ref=last_out, dst_ref=last_in.at[mx], send_sem=last_send.at[d - 1], recv_sem=last_recv.at[d - 1],
            device_id=(me, lax.rem(mx + d, nx)), device_id_type=MESH,
        )

    for d in range(1, nx):
        last_copy(d).start()

    def write(h):
        return pltpu.make_async_copy(
            ypart.at[h], basis_out.at[:, pl.ds(h * prows, prows)], out_sem.at[h]
        )

    for q in range(nx):
        some = range(q * PIECES, (q + 1) * PIECES)
        value = jnp.concatenate([yfull[ITERS % 2, h] for h in some], axis=1)
        value = exact(factor_y[...], value) * math.sqrt(total_rows)
        for h in some:
            ypart[h] = value[:, h % PIECES * prows : (h % PIECES + 1) * prows]
            write(h).start()

    for d in range(1, nx):
        last_copy(d).wait()
    total = last_in[0]
    for x in range(1, nx):
        total = total + last_in[x]
    factor = inverse_factor(total[:, MODES : MODES + R])
    second_out[...] = exact(factor, sketched) * math.sqrt(unfold_rows)
    rest_out[...] = exact(factor, total[:, :MODES]) / math.sqrt(unfold_rows)
    for h in range(pieces):
        write(h).wait()


def move(basis, second, rest, basis_out, second_out, rest_out, held, held_second, held_rest, sem, out_sem):
    width = basis.shape[1] // MOVES
    spans = [pl.ds(n * width, width) for n in range(MOVES)]
    ways = [(basis.at[:, at], held.at[:, at], basis_out.at[:, at]) for at in spans]
    ways += [(second, held_second, second_out), (rest, held_rest, rest_out)]
    ins = [pltpu.make_async_copy(a, b, sem.at[n]) for n, (a, b, c) in enumerate(ways)]
    outs = [pltpu.make_async_copy(b, c, out_sem.at[n]) for n, (a, b, c) in enumerate(ways)]
    for copy in ins:
        copy.start()
    for one, other in zip(ins, outs):
        one.wait()
        other.start()
    for copy in outs:
        copy.wait()


def solution(mesh):
    ns, nx = mesh.shape["space"], mesh.shape["param"]

    def shards(snapshots, sketch, following):
        rows, columns = snapshots.shape
        pieces = PIECES * nx
        prows = rows // pieces
        per = R // ns
        slices = columns // MODES
        steps = ITERS + 1
        dma = pltpu.SemaphoreType.DMA
        made = pl.pallas_call(
            functools.partial(kernel, ns, nx, rows * ns, slices * R * nx),
            out_shape=(
                jax.ShapeDtypeStruct((R, rows), F32),
                jax.ShapeDtypeStruct((R, slices * R), F32),
                jax.ShapeDtypeStruct((R, MODES), F32),
            ),
            in_specs=[pl.BlockSpec(memory_space=pl.ANY)] * 3,
            out_specs=(
                pl.BlockSpec(memory_space=pl.ANY),
                pl.BlockSpec(memory_space=pltpu.VMEM),
                pl.BlockSpec(memory_space=pltpu.VMEM),
            ),
            scratch_shapes=[
                pltpu.VMEM((R, columns), F32),
                pltpu.VMEM((R, MODES), F32),
                pltpu.VMEM((pieces, prows, columns), BF16),
                pltpu.VMEM((pieces, prows, columns), BF16),
                pltpu.VMEM((2 * nx, columns, rows // (2 * nx)), BF16),
                pltpu.VMEM((2 * nx, columns, rows // (2 * nx)), BF16),
                pltpu.VMEM((4, prows, columns), F32),
                pltpu.VMEM((2 * R, columns), BF16),
                pltpu.VMEM((pieces, R, prows), F32),
                pltpu.VMEM((2, 2, PIECES // 2, R, prows), F32),
                pltpu.VMEM((2, 2, PIECES, R, prows), F32),
                pltpu.VMEM((2, pieces, R, prows), F32),
                pltpu.VMEM((R, columns), F32),
                pltpu.VMEM((R, columns), F32),
                pltpu.VMEM((ns, per, 8, 128), F32),
                pltpu.VMEM((steps, ns, per, 8, 128), F32),
                pltpu.VMEM((steps, ns, per, 8, 128), F32),
                pltpu.VMEM((steps, nx, 8, 128), F32),
                pltpu.VMEM((steps, nx, 8, 128), F32),
                pltpu.VMEM((steps, ns, 8, 128), F32),
                pltpu.VMEM((R, MODES + 128), F32),
                pltpu.VMEM((nx, R, MODES + 128), F32),
                pltpu.VMEM((R, R), F32),
                dma((2,)),
                dma((4,)),
                dma((36,)),
                dma((steps, 36)),
                dma,
                dma((steps,)),
                dma,
                dma((steps,)),
                dma((nx - 1,)),
                dma((steps, nx - 1)),
                dma((nx - 1,)),
                dma((steps, nx - 1)),
                dma,
                dma((steps,)),
                dma((nx - 1,)),
                dma((nx - 1,)),
                dma((pieces,)),
            ],
            compiler_params=pltpu.CompilerParams(
                collective_id=0, has_side_effects=True, vmem_limit_bytes=60 * 1024 * 1024
            ),
        )(snapshots, sketch.T, following.T)
        anywhere = pl.BlockSpec(memory_space=pl.ANY)
        return pl.pallas_call(
            move,
            out_shape=tuple(jax.ShapeDtypeStruct(one.shape, F32) for one in made),
            in_specs=[anywhere] * 3,
            out_specs=(anywhere,) * 3,
            scratch_shapes=[pltpu.VMEM(one.shape, F32) for one in made] + [dma((MOVES + 2,)), dma((MOVES + 2,))],
        )(*made)

    return jax.shard_map(
        shards,
        mesh=mesh,
        in_specs=(P("space", "param"), P("param", None), P()),
        out_specs=(P(None, "space"), P(None, "param"), P()),
        check_vma=False,
    )
```

```python
import functools
import math

import jax
import jax.numpy as jnp
from jax import lax
from jax.experimental import pallas as pl
from jax.experimental.pallas import tpu as pltpu
from jax.sharding import PartitionSpec as P

MESH = pl.DeviceIdType.MESH
R = 32
MOVES = 4
MODES = 256
ITERS = 3
BLOCK = 8
PIECES = 6
F32, BF16 = jnp.float32, jnp.bfloat16
NN = (((1,), (0,)), ((), ()))
NT = (((1,), (1,)), ((), ()))


def exact(a, b, dims=NN):
    return lax.dot_general(a, b, dims, precision=lax.Precision.HIGHEST, preferred_element_type=F32)


def split(value):
    high = value.astype(BF16)
    low = (value - high.astype(F32)).astype(BF16)
    return jnp.concatenate([high, low], axis=0)


def fold(pair):
    return pair[:R] + pair[R:]


def gram_of(stacked):
    both = lax.dot_general(stacked, stacked, NT, preferred_element_type=F32)
    half = fold(both)
    return half[:, :R] + half[:, R:]


def inverse_factor(gram):
    wide = (R, 2 * R)
    rows = lax.broadcasted_iota(jnp.int32, (R, R), 0)
    columns = lax.broadcasted_iota(jnp.int32, (R, R), 1)
    eye = jnp.where(rows == columns, 1.0, 0.0).astype(F32)
    work = jnp.concatenate([gram, eye], axis=1)
    below = lax.broadcasted_iota(jnp.int32, wide, 0)
    for j in range(0, R, BLOCK):
        row = [work[j + i : j + i + 1, :] for i in range(BLOCK)]
        spread = [[jnp.broadcast_to(row[i][:, j + k : j + k + 1], (1, 2 * R)) for k in range(BLOCK)] for i in range(BLOCK)]
        column = [jnp.broadcast_to(work[:, j + i : j + i + 1], wide) for i in range(BLOCK)]
        for i in range(BLOCK):
            if j + i == R - 1:
                break
            inverse = 1.0 / spread[i][i]
            scaled = row[i] * inverse
            work = work - jnp.where(below > j + i, column[i], 0.0) * scaled
            for k in range(i + 1, BLOCK):
                ratio = spread[i][k] * inverse
                row[k] = row[k] - spread[i][k] * scaled
                column[k] = column[k] - column[i] * ratio
                for m in range(k, BLOCK):
                    spread[k][m] = spread[k][m] - spread[i][m] * ratio
    diagonal = jnp.sum(jnp.where(rows == columns, work[:, :R], 0.0), axis=1, keepdims=True)
    return work[:, R:] / jnp.sqrt(diagonal)


def pack(square):
    return jnp.concatenate([square[8 * i : 8 * i + 8] for i in range(4)], axis=1)


def unpack(tile):
    return jnp.concatenate([tile[:, R * i : R * i + R] for i in range(4)], axis=0)


def kernel(
    ns, nx, total_rows, unfold_rows,
    snap, sketch_in, following_in, basis_out, second_out, rest_out,
    sketch, following, high, low, high_t, low_t, stage, zst, ypart, first_in, second_in, yfull, zacc, zfull,
    tiles_out, tiles_in, sums, gram_in, own_in, space_in, last_out, last_in,
    factor_y,
    small_sem, load_sem, send_sem, recv_sem, tile_send, tile_recv, sum_send, sum_recv,
    gram_send, gram_recv, own_send, own_recv, space_send, space_recv, last_send, last_recv, out_sem,
):
    me, mx = lax.axis_index("space"), lax.axis_index("param")
    right, left, across = lax.rem(mx + 1, nx), lax.rem(mx + nx - 1, nx), lax.rem(mx + 2, nx)
    pieces, prows, columns = high.shape
    per = tiles_out.shape[1]
    third = PIECES // 2
    loads = stage.shape[0]

    def part(quarter, piece):
        return quarter * PIECES + piece

    steps = range(third)
    far = [part(across, k + side * third) for k in steps for side in (0, 1)]
    plain = [h for k in steps for h in (part(right, k + third), part(left, k))]
    merged = [h for k in steps for h in (part(right, k), part(left, k + third))]
    own = [part(mx, k + side * third) for k in steps for side in (0, 1)]
    order = far + plain + merged + own
    quarters = [across] * 6 + [right, left] * 6 + [mx] * 6
    sides = [0, 1] * third + [1, 0] * third + [0, 1] * third * 2
    places = [(quarters[n] * 2 + sides[n], n % 6 // 2) for n in range(4 * PIECES)]

    def load(n):
        return pltpu.make_async_copy(
            snap.at[pl.ds(pl.multiple_of(order[n] * prows, prows), prows), :],
            stage.at[n % loads], load_sem.at[n % loads],
        )

    small = [
        pltpu.make_async_copy(sketch_in, sketch, small_sem.at[0]),
        pltpu.make_async_copy(following_in, following, small_sem.at[1]),
    ]
    small[0].start()
    for n in range(loads):
        load(n).start()
    small[1].start()

    barrier = pltpu.get_barrier_semaphore()

    def greet(d, carry):
        pl.semaphore_signal(barrier, inc=1, device_id=(lax.rem(me + d, ns), mx), device_id_type=MESH)
        return carry

    lax.fori_loop(1, ns, greet, 0)
    for d in range(1, nx):
        pl.semaphore_signal(barrier, inc=1, device_id=(me, lax.rem(mx + d, nx)), device_id_type=MESH)

    small[0].wait()
    zst[...] = split(sketch[...])

    def product(n, first):
        h = order[n]
        if first:
            load(n).wait()
            value = stage[n % loads]
            top = value.astype(BF16)
            rest = (value - top.astype(F32)).astype(BF16)
            high[h] = top
            low[h] = rest
            pair = lax.dot_general(zst[...], top, NT, preferred_element_type=F32)
            pair += lax.dot_general(zst[...], rest, NT, preferred_element_type=F32)
            if n + loads < pieces:
                load(n + loads).start()
        else:
            side, k = places[n]
            at = pl.ds(k * prows, prows)
            pair = lax.dot_general(zst[...], high_t[side, :, at], NN, preferred_element_type=F32)
            pair += lax.dot_general(zst[...], low_t[side, :, at], NN, preferred_element_type=F32)
        return fold(pair)

    def turn(source, target):
        def one(i, carry):
            for b in range(columns // 256):
                at = pl.ds(b * 256, 256)
                rows = [source[i * third + k, :, at] for k in steps]
                target[i, at, :] = jnp.concatenate(rows, axis=0).T
            return carry

        lax.fori_loop(0, pieces // third, one, 0)

    def in_turn(numbers, first, ready):
        ahead = None
        for n in numbers:
            value = product(n, first)
            if ahead is not None:
                ready(*ahead)
            ahead = (n, value)
        ready(*ahead)

    def along_x(source, target, n, it, x):
        return pltpu.make_async_remote_copy(
            src_ref=source, dst_ref=target, send_sem=send_sem.at[n], recv_sem=recv_sem.at[it, n],
            device_id=(me, x), device_id_type=MESH,
        )

    def accumulate(it, some, last=False):
        stacked = [split(yfull[it, h]) for h in some]
        for b in range(columns // 256):
            at = pl.ds(b * 256, 256)
            pair = None
            for a, h in zip(stacked, some):
                one = lax.dot_general(a, high[h, :, at], NN, preferred_element_type=F32)
                one += lax.dot_general(a, low[h, :, at], NN, preferred_element_type=F32)
                pair = one if pair is None else pair + one
            if not last:
                zacc[:, at] += fold(pair)
                continue
            total = zacc[:, at] + fold(pair)
            for g in (2 * b, 2 * b + 1):
                block = total[:, g % 2 * 128 : g % 2 * 128 + 128].reshape(4, 8, 128)
                for t in range(4):
                    tiles_out[(g * 4 + t) // per, (g * 4 + t) % per] = block[t]
        return stacked

    def peer_copy(ref, it, d, send, recv):
        return pltpu.make_async_remote_copy(
            src_ref=ref.at[it, mx], dst_ref=ref.at[it, mx], send_sem=send.at[d - 1], recv_sem=recv.at[it, d - 1],
            device_id=(me, lax.rem(mx + d, nx)), device_id_type=MESH,
        )

    nc = 2
    nz = min(4, ns // nc)
    ny = ns // (nc * nz)
    myy, myz, myc = me // (nz * nc), me // nc % nz, me % nc
    hops = sorted(
        (-min(dy, ny - dy) - min(dz, nz - dz), dy, dz, dc)
        for dy in range(ny) for dz in range(nz) for dc in range(nc) if dy or dz or dc
    )
    others = [
        ((lax.rem(myy + dy, ny) * nz + lax.rem(myz + dz, nz)) * nc + lax.rem(myc + dc, nc)) for _, dy, dz, dc in hops
    ]

    def start_space(source, ref, it, send, recv):
        for s in others:
            pltpu.make_async_remote_copy(
                src_ref=source(s), dst_ref=ref.at[it, me], send_sem=send, recv_sem=recv.at[it],
                device_id=(s, mx), device_id_type=MESH,
            ).start()

    def all_but_one(ref, it, sem):
        some = ref.at[it, pl.ds(0, ns - 1)]
        pltpu.make_async_copy(some, some, sem).wait()

    def sum_of(ref, it, count):
        total = ref[it, 0]
        for x in range(1, count):
            total = total + ref[it, x]
        return total

    def iteration(it, first):
        now = it % 2
        far_copies, plain_copies, merged_copies = {}, {}, []

        def send_far(n, value):
            k, side = divmod(n, 2)
            if not first:
                ypart[order[n]] = value
            copy = along_x(ypart.at[order[n]], first_in.at[now, side, k], n, it, left if side else right)
            copy.start()
            far_copies[n] = copy

        def send_plain(n, value):
            k, side = divmod(n - len(far), 2)
            ypart[order[n]] = value
            slot = second_in.at[now, side, k if side else k + third]
            copy = along_x(ypart.at[order[n]], slot, n, it, left if side else right)
            copy.start()
            plain_copies[n - len(far)] = copy

        def keep(n, value):
            ypart[order[n]] = value

        begun, base = len(far) + len(plain), pieces - len(own)
        if first:
            in_turn(range(len(far)), first, keep)
            pl.semaphore_wait(barrier, ns - 1 + nx - 1)
            for n in range(len(far)):
                send_far(n, None)
        else:
            in_turn(range(2), first, send_far)
            gram_in[it, mx] = pack(gram_of(zst[...]))
            for d in range(1, nx):
                peer_copy(gram_in, it, d, gram_send, gram_recv).start()
            in_turn(range(2, len(far)), first, send_far)
        in_turn(range(len(far), begun), first, send_plain)
        in_turn(range(begun, base), first, keep)
        for m, h in enumerate(merged):
            k, side = divmod(m, 2)
            far_copies[m].wait_recv()
            ypart[h] += first_in[now, side, k]
            slot = second_in.at[now, side, k + third if side else k]
            copy = along_x(ypart.at[h], slot, begun + m, it, left if side else right)
            copy.start()
            merged_copies.append(copy)

        if first:
            factor = None
        else:
            for d in range(1, nx):
                peer_copy(gram_in, it, d, gram_send, gram_recv).wait()
            factor = inverse_factor(unpack(sum_of(gram_in, it, nx)))
        in_turn(range(base, pieces), first, keep)

        spread = []

        def send_own(h, n, x):
            copy = along_x(yfull.at[now, h], yfull.at[now, h], n, it, x)
            copy.start()
            spread.append(copy)
            return copy

        straight, turned, values = [], [], []

        def cross(k):
            for m in (2 * k, 2 * k + 1):
                turned.append(send_own(own[m], 24 + m, right if m % 2 else left))

        for k in steps:
            value = []
            for m in (2 * k, 2 * k + 1):
                merged_copies[m].wait_recv()
                plain_copies[m].wait_recv()
            for m in (2 * k, 2 * k + 1):
                piece = k + m % 2 * third
                value.append(ypart[own[m]] + second_in[now, 0, piece] + second_in[now, 1, piece])
            value = jnp.concatenate(value, axis=1)
            if factor is not None:
                value = exact(factor, value)
            values.append(value)
            for m in (2 * k, 2 * k + 1):
                yfull[now, own[m]] = value[:, m % 2 * prows : (m % 2 + 1) * prows]
                straight.append(send_own(own[m], 18 + m, left if m % 2 else right))
        own_in[it, mx] = pack(gram_of(split(jnp.concatenate(values, axis=1))))
        for d in range(1, nx):
            peer_copy(own_in, it, d, own_send, own_recv).start()
        for k in steps:
            cross(k)
        zacc[...] = jnp.zeros_like(zacc)
        accumulate(now, own)
        onward = []
        for k in steps:
            straight[2 * k].wait_recv()
            onward.append(send_own(part(left, k), 30 + 2 * k, right))
            straight[2 * k + 1].wait_recv()
            onward.append(send_own(part(right, k + third), 31 + 2 * k, left))
        accumulate(now, [h for k in steps for h in (part(left, k), part(right, k + third))])

        for d in range(1, nx):
            peer_copy(own_in, it, d, own_send, own_recv).wait()
        space_in[it, me] = sum_of(own_in, it, nx)
        start_space(lambda s: space_in.at[it, me], space_in, it, space_send, space_recv)

        for k in steps:
            turned[2 * k].wait_recv()
            turned[2 * k + 1].wait_recv()
            accumulate(now, [part(right, k), part(left, k + third)])
        for k in steps:
            onward[2 * k].wait_recv()
            onward[2 * k + 1].wait_recv()
            accumulate(now, [part(across, k), part(across, k + third)], k == third - 1)

        start_space(lambda s: tiles_out.at[s], tiles_in, it, tile_send, tile_recv)
        tiles_in[it, me] = tiles_out[me]

        if first:
            turn(high, high_t)
        all_but_one(space_in, it, space_recv.at[it])
        factor_y[...] = inverse_factor(unpack(sum_of(space_in, it, ns)))
        all_but_one(space_in, it, space_send)
        for copy in [*far_copies.values(), *plain_copies.values(), *merged_copies, *spread]:
            copy.wait_send()

        all_but_one(tiles_in, it, tile_recv.at[it])
        sums[it, me] = sum_of(tiles_in, it, ns)
        start_space(lambda s: sums.at[it, me], sums, it, sum_send, sum_recv)
        all_but_one(tiles_in, it, tile_send)
        if first:
            turn(low, low_t)
        all_but_one(sums, it, sum_recv.at[it])
        gathered, blocks = sums[it].reshape(R, 8, 128), []
        for g in range(columns // 128):
            block = gathered[g * 4 : g * 4 + 4].reshape(R, 128)
            blocks.append(block)
        whole = exact(factor_y[...], jnp.concatenate(blocks, axis=1))
        zst[...] = split(whole)
        zfull[...] = whole
        all_but_one(sums, it, sum_send)

    iteration(0, True)

    def later(it, carry):
        iteration(it, False)
        return carry

    lax.fori_loop(1, ITERS + 1, later, 0)

    small[1].wait()
    slices = columns // MODES
    zfull[...] = zfull[...] * (1.0 / math.sqrt(total_rows))
    sketched, rest = [], jnp.zeros((R, MODES), F32)
    for i in range(slices):
        block = zfull[:, pl.ds(i * MODES, MODES)]
        one = exact(following[...], block, NT)
        rest = rest + exact(one, block)
        sketched.append(one)
    sketched = jnp.concatenate(sketched, axis=1)
    last_out[:, pl.ds(0, MODES)] = rest
    last_out[:, pl.ds(MODES, 128)] = jnp.concatenate(
        [exact(sketched, sketched, NT), jnp.zeros((R, 128 - R), F32)], axis=1
    )
    last_in[mx] = last_out[...]

    def last_copy(d):
        return pltpu.make_async_remote_copy(
            src_ref=last_out, dst_ref=last_in.at[mx], send_sem=last_send.at[d - 1], recv_sem=last_recv.at[d - 1],
            device_id=(me, lax.rem(mx + d, nx)), device_id_type=MESH,
        )

    for d in range(1, nx):
        last_copy(d).start()

    def write(h):
        return pltpu.make_async_copy(
            ypart.at[h], basis_out.at[:, pl.ds(h * prows, prows)], out_sem.at[h]
        )

    for q in range(nx):
        some = range(q * PIECES, (q + 1) * PIECES)
        value = jnp.concatenate([yfull[ITERS % 2, h] for h in some], axis=1)
        value = exact(factor_y[...], value) * math.sqrt(total_rows)
        for h in some:
            ypart[h] = value[:, h % PIECES * prows : (h % PIECES + 1) * prows]
            write(h).start()

    for d in range(1, nx):
        last_copy(d).wait()
    total = last_in[0]
    for x in range(1, nx):
        total = total + last_in[x]
    factor = inverse_factor(total[:, MODES : MODES + R])
    second_out[...] = exact(factor, sketched) * math.sqrt(unfold_rows)
    rest_out[...] = exact(factor, total[:, :MODES]) / math.sqrt(unfold_rows)
    for h in range(pieces):
        write(h).wait()


def move(basis, second, rest, basis_out, second_out, rest_out, held, held_second, held_rest, sem, out_sem):
    width = basis.shape[1] // MOVES
    spans = [pl.ds(n * width, width) for n in range(MOVES)]
    ways = [(basis.at[:, at], held.at[:, at], basis_out.at[:, at]) for at in spans]
    ways += [(second, held_second, second_out), (rest, held_rest, rest_out)]
    ins = [pltpu.make_async_copy(a, b, sem.at[n]) for n, (a, b, c) in enumerate(ways)]
    outs = [pltpu.make_async_copy(b, c, out_sem.at[n]) for n, (a, b, c) in enumerate(ways)]
    for copy in ins:
        copy.start()
    for one, other in zip(ins, outs):
        one.wait()
        other.start()
    for copy in outs:
        copy.wait()


def solution(mesh):
    ns, nx = mesh.shape["space"], mesh.shape["param"]

    def shards(snapshots, sketch, following):
        rows, columns = snapshots.shape
        pieces = PIECES * nx
        prows = rows // pieces
        per = R // ns
        slices = columns // MODES
        steps = ITERS + 1
        dma = pltpu.SemaphoreType.DMA
        made = pl.pallas_call(
            functools.partial(kernel, ns, nx, rows * ns, slices * R * nx),
            out_shape=(
                jax.ShapeDtypeStruct((R, rows), F32),
                jax.ShapeDtypeStruct((R, slices * R), F32),
                jax.ShapeDtypeStruct((R, MODES), F32),
            ),
            in_specs=[pl.BlockSpec(memory_space=pl.ANY)] * 3,
            out_specs=(
                pl.BlockSpec(memory_space=pl.ANY),
                pl.BlockSpec(memory_space=pltpu.VMEM),
                pl.BlockSpec(memory_space=pltpu.VMEM),
            ),
            scratch_shapes=[
                pltpu.VMEM((R, columns), F32),
                pltpu.VMEM((R, MODES), F32),
                pltpu.VMEM((pieces, prows, columns), BF16),
                pltpu.VMEM((pieces, prows, columns), BF16),
                pltpu.VMEM((2 * nx, columns, rows // (2 * nx)), BF16),
                pltpu.VMEM((2 * nx, columns, rows // (2 * nx)), BF16),
                pltpu.VMEM((4, prows, columns), F32),
                pltpu.VMEM((2 * R, columns), BF16),
                pltpu.VMEM((pieces, R, prows), F32),
                pltpu.VMEM((2, 2, PIECES // 2, R, prows), F32),
                pltpu.VMEM((2, 2, PIECES, R, prows), F32),
                pltpu.VMEM((2, pieces, R, prows), F32),
                pltpu.VMEM((R, columns), F32),
                pltpu.VMEM((R, columns), F32),
                pltpu.VMEM((ns, per, 8, 128), F32),
                pltpu.VMEM((steps, ns, per, 8, 128), F32),
                pltpu.VMEM((steps, ns, per, 8, 128), F32),
                pltpu.VMEM((steps, nx, 8, 128), F32),
                pltpu.VMEM((steps, nx, 8, 128), F32),
                pltpu.VMEM((steps, ns, 8, 128), F32),
                pltpu.VMEM((R, MODES + 128), F32),
                pltpu.VMEM((nx, R, MODES + 128), F32),
                pltpu.VMEM((R, R), F32),
                dma((2,)),
                dma((4,)),
                dma((36,)),
                dma((steps, 36)),
                dma,
                dma((steps,)),
                dma,
                dma((steps,)),
                dma((nx - 1,)),
                dma((steps, nx - 1)),
                dma((nx - 1,)),
                dma((steps, nx - 1)),
                dma,
                dma((steps,)),
                dma((nx - 1,)),
                dma((nx - 1,)),
                dma((pieces,)),
            ],
            compiler_params=pltpu.CompilerParams(
                collective_id=0, has_side_effects=True, vmem_limit_bytes=60 * 1024 * 1024
            ),
        )(snapshots, sketch.T, following.T)
        anywhere = pl.BlockSpec(memory_space=pl.ANY)
        return pl.pallas_call(
            move,
            out_shape=tuple(jax.ShapeDtypeStruct(one.shape, F32) for one in made),
            in_specs=[anywhere] * 3,
            out_specs=(anywhere,) * 3,
            scratch_shapes=[pltpu.VMEM(one.shape, F32) for one in made] + [dma((MOVES + 2,)), dma((MOVES + 2,))],
        )(*made)

    return jax.shard_map(
        shards,
        mesh=mesh,
        in_specs=(P("space", "param"), P("param", None), P()),
        out_specs=(P(None, "space"), P(None, "param"), P()),
        check_vma=False,
    )
```
